128 devices in a mesh: row: 16 (over x, z), col: 8 (over y, core).
Axes of the slice: x: 4, y: 4, z: 4, core: 2. Of those that a mesh axis runs over, the one named last changes fastest.
Arguments:
- rhs_first: bfloat16 [2, 2048, 1024], P(None, 'row', 'col'), may hold values from -6 to 6
- rhs_last: bfloat16 [2, 2048, 1024], P(None, 'row', 'col'), may hold values from -6 to 6
- inv_first: bfloat16 [2, 2048, 2048], P(None, 'row', 'col'), may hold values from -0.09375 to 0.09375
- coupling: bfloat16 [2, 2048, 2048], P(None, 'row', 'col'), may hold values from -0.09375 to 0.09375
- inv_last: bfloat16 [2, 2048, 2048], P(None, 'row', 'col'), may hold values from -0.09375 to 0.09375
- earlier: bfloat16 [2, 49152, 1024], P(None, 'row', 'col'), may hold values from -6 to 6
- patch_old: int32 [49152], P('row'), may hold values from 0 to 4095
- weight_old: bfloat16 [49152], P('row'), may hold values from -4 to 4
- patch_new: int32 [2, 2048], P(None, 'row'), may hold values from 0 to 4095
- weight_new: bfloat16 [2, 2048], P(None, 'row'), may hold values from -4 to 4
- stress_map: bfloat16 [2, 16384, 4096], P(None, 'row', 'col'), may hold values from -0.03125 to 0.03125
Outputs:
- pressures: bfloat16 [2, 2, 2048, 1024], P(None, None, 'row', 'col')
- stress_rao: bfloat16 [2, 16384, 1024], P(None, 'row', 'col')
The draws below stay inside these ranges and needn't reach their ends.
All inputs are finite; a program needn't handle non-finite values.
Results may differ from the reference program's by a relative error of at most 0.006.
Values may be sent and summed in bfloat16 or wider, within the bound.
No kernel may reach another device: no remote copies, remote signals or barrier semaphores. Data moves between devices by JAX's collectives and lax.ppermute only.
A program may use at most 128 MiB of HBM per device.

```python
import jax
import jax.numpy as jnp

NB = 2048
RS = 1024
PAN_OLD = 49152
PATCHES = 4096
HOT = 16384


def plant(array, stream_key, least, largest):
    longest = array.shape.index(max(array.shape))
    spots = []
    for shift in (0, 1):
        where = [jax.random.randint(jax.random.fold_in(stream_key, axis), (), 0, length) for axis, length in enumerate(array.shape)]
        where[longest] = (where[longest] + shift) % array.shape[longest]
        spots.append(tuple(where))
    return array.at[spots[0]].set(least).at[spots[1]].set(largest)


def shard_levels(key, dims, pieces, least, largest):
    def one(dim, parts):
        draws = jax.random.uniform(jax.random.fold_in(jax.random.fold_in(key, 6), dim), (parts,), jnp.float32, least / len(pieces), largest / len(pieces))
        return jnp.repeat(jnp.exp(draws), dims[dim] // parts).reshape((-1,) + (1,) * (len(dims) - dim - 1))

    level = one(*pieces[0])
    for cut in pieces[1:]:
        level = level * one(*cut)
    return level


def bell_draw(key, extent, scale, bound, cuts=(), kind=jnp.bfloat16):
    factor_of = shard_levels(key, extent, cuts, -0.22, 0.18) if cuts else 1.0
    values = jax.random.normal(key, extent, jnp.float32) * scale * factor_of
    return jnp.minimum(jnp.maximum(values, -bound), bound).astype(kind)


def setup_inputs(seed: int = 0) -> dict:
    arg_keys = jax.random.split(jax.random.key(seed), 12)
    rhs_first = bell_draw(arg_keys[0], (2, NB, RS), 1.0, 6.0, ((1, 16), (2, 8)))
    rhs_last = bell_draw(arg_keys[1], (2, NB, RS), 1.0, 6.0, ((1, 16), (2, 8)))
    inv_first = bell_draw(arg_keys[2], (2, NB, NB), (2 * NB) ** -0.5, 0.09375, ((1, 16), (2, 8)))
    coupling = bell_draw(arg_keys[3], (2, NB, NB), (2 * NB) ** -0.5, 0.09375, ((1, 16), (2, 8)))
    inv_last = bell_draw(arg_keys[4], (2, NB, NB), (2 * NB) ** -0.5, 0.09375, ((1, 16), (2, 8)))
    earlier = bell_draw(arg_keys[5], (2, PAN_OLD, RS), 1.0, 6.0, ((1, 16), (2, 8)))
    patch_old = plant(jax.random.randint(arg_keys[6], (PAN_OLD,), 0, PATCHES), jax.random.fold_in(arg_keys[6], 1), 0, PATCHES - 1).astype(jnp.int32)
    weight_old = bell_draw(arg_keys[7], (PAN_OLD,), 1.0, 4.0, ((0, 16),))
    patch_new = plant(jax.random.randint(arg_keys[8], (2, NB), 0, PATCHES), jax.random.fold_in(arg_keys[8], 1), 0, PATCHES - 1).astype(jnp.int32)
    weight_new = bell_draw(arg_keys[9], (2, NB), 1.0, 4.0, ((1, 16),))
    stress_map = bell_draw(arg_keys[10], (2, HOT, PATCHES), (10 * PATCHES) ** -0.5, 0.03125, ((1, 16), (2, 8)))
    return dict(rhs_first=rhs_first, rhs_last=rhs_last, inv_first=inv_first, coupling=coupling, inv_last=inv_last, earlier=earlier, patch_old=patch_old, weight_old=weight_old, patch_new=patch_new, weight_new=weight_new, stress_map=stress_map)


def complex_dot(matrix, vectors):
    real_real = jnp.dot(matrix[0], vectors[0], preferred_element_type=jnp.float32)
    imag_imag = jnp.dot(matrix[1], vectors[1], preferred_element_type=jnp.float32)
    real_imag = jnp.dot(matrix[0], vectors[1], preferred_element_type=jnp.float32)
    imag_real = jnp.dot(matrix[1], vectors[0], preferred_element_type=jnp.float32)
    return jnp.stack([real_real - imag_imag, real_imag + imag_real])


def reference(rhs_first, rhs_last, inv_first, coupling, inv_last, earlier, patch_old, weight_old, patch_new, weight_new, stress_map):
    x_first = complex_dot(inv_first, rhs_first).astype(jnp.bfloat16)
    reduced = (rhs_last.astype(jnp.float32) - complex_dot(coupling, x_first)).astype(jnp.bfloat16)
    x_last = complex_dot(inv_last, reduced).astype(jnp.bfloat16)
    pressures = jnp.stack([x_first, x_last])
    pressures_all = jnp.concatenate([earlier, x_first, x_last], axis=1)
    patch_ids = jnp.concatenate([patch_old, patch_new[0], patch_new[1]]).astype(jnp.int32)
    panel_weights = jnp.concatenate([weight_old, weight_new[0], weight_new[1]]).astype(jnp.float32)
    weighted = panel_weights[None, :, None] * pressures_all.astype(jnp.float32)
    real_loads = jax.ops.segment_sum(weighted[0], patch_ids, num_segments=PATCHES)
    imag_loads = jax.ops.segment_sum(weighted[1], patch_ids, num_segments=PATCHES)
    patch_loads = jnp.stack([real_loads, imag_loads]).astype(jnp.bfloat16)
    stress_rao = complex_dot(stress_map, patch_loads).astype(jnp.bfloat16)
    return pressures, stress_rao
```

```python
import functools

import jax
import jax.numpy as jnp
from jax import lax
from jax.experimental import pallas as pl
from jax.experimental.pallas import tpu as pltpu
from jax.sharding import PartitionSpec as P

PATCHES = 4096
ROWS = 16
COLS = 8
BF16 = jnp.bfloat16
F32 = jnp.float32
PARAMS = pltpu.CompilerParams(vmem_limit_bytes=48 * 2**20)


def weighted_onehot(ids, weights, first, count):
    patch = lax.broadcasted_iota(jnp.int32, (count, ids.shape[1]), 0)
    return jnp.where(patch == ids - first, weights, jnp.zeros((), BF16))


def old_loads_kernel(ids_ref, weights_ref, earlier_ref, out_ref, side, *, tile, chunk):
    step = pl.program_id(0)

    @pl.when(step == 0)
    def _():
        side[:, :128] = earlier_ref[0]
        side[:, 128:] = earlier_ref[1]

    total = jnp.zeros((tile, 256), F32)
    for start in range(0, side.shape[0], chunk):
        panels = slice(start, start + chunk)
        onehot = weighted_onehot(ids_ref[:, panels], weights_ref[:, panels], step * tile, tile)
        total += jnp.dot(onehot, side[panels], preferred_element_type=F32)
    for block in range(tile // 256):
        rows = slice(block * 256, (block + 1) * 256)
        out_ref[block, :256] = total[rows, :128].astype(BF16)
        out_ref[block, 256:] = total[rows, 128:].astype(BF16)


def old_loads(ids, weights, earlier):
    panels = earlier.shape[1]
    tile = 1024
    whole = lambda step: (0, 0)
    return pl.pallas_call(
        functools.partial(old_loads_kernel, tile=tile, chunk=512),
        out_shape=jax.ShapeDtypeStruct((ROWS, 512, 128), BF16),
        grid=(PATCHES // tile,),
        in_specs=[
            pl.BlockSpec((1, panels), whole),
            pl.BlockSpec((1, panels), whole),
            pl.BlockSpec((2, panels, 128), lambda step: (0, 0, 0)),
        ],
        out_specs=pl.BlockSpec((tile // 256, 512, 128), lambda step: (step, 0, 0)),
        scratch_shapes=[pltpu.VMEM((panels, 256), BF16)],
        compiler_params=PARAMS,
        name="old_loads",
    )(ids, weights, earlier)


def sum_loads_kernel(parts_ref, out_ref):
    total = parts_ref[0].astype(F32)
    for source in range(1, ROWS):
        total += parts_ref[source].astype(F32)
    total = total.astype(BF16)
    for target in range(ROWS):
        out_ref[target] = total


def sum_loads(parts):
    return pl.pallas_call(
        sum_loads_kernel,
        out_shape=jax.ShapeDtypeStruct(parts.shape, BF16),
        compiler_params=PARAMS,
        name="sum_loads",
    )(parts)


def rows_kernel(order_ref, own_matrix_ref, other_matrix_ref, gathered_ref, *rest, pick, subtract, extra):
    rest = list(rest)
    base_ref = rest.pop(0) if subtract else None
    extra_ref = rest.pop(0) if extra else None
    own_ref, copies_ref, side = rest
    for source in range(ROWS):
        rows = slice(source * 128, (source + 1) * 128)
        side[rows, :128] = gathered_ref[source, :128]
        side[rows, 128:] = gathered_ref[source, 128:256]
    real = jnp.zeros((128, 256), F32)
    imag = jnp.zeros((128, 256), F32)
    for core, matrix_ref in enumerate((own_matrix_ref, other_matrix_ref)):
        for hop in range(4):
            block = order_ref[core * 4 + hop]
            part = side[pl.ds(pl.multiple_of(block * 256, 256), 256)]
            real += jnp.dot(matrix_ref[hop, pick, 0], part, preferred_element_type=F32)
            imag += jnp.dot(matrix_ref[hop, pick, 1], part, preferred_element_type=F32)
    out_real = real[:, :128] - imag[:, 128:]
    out_imag = real[:, 128:] + imag[:, :128]
    if subtract:
        out_real = base_ref[0].astype(F32) - out_real
        out_imag = base_ref[1].astype(F32) - out_imag
    out_real = out_real.astype(BF16)
    out_imag = out_imag.astype(BF16)
    own_ref[0] = out_real
    own_ref[1] = out_imag
    for target in range(ROWS):
        copies_ref[target, :128] = out_real
        copies_ref[target, 128:256] = out_imag
        if extra:
            copies_ref[target, 256:] = extra_ref[...]


def rows_product(name, order, matrix, pick, gathered, base=None, extra=None):
    vmem = pl.BlockSpec(memory_space=pltpu.VMEM)
    operands = [*matrix, gathered]
    operands += [value for value in (base, extra) if value is not None]
    height = 256 if extra is None else 256 + extra.shape[0]
    return pl.pallas_call(
        functools.partial(
            rows_kernel, pick=pick, subtract=base is not None, extra=extra is not None
        ),
        out_shape=(
            jax.ShapeDtypeStruct((2, 128, 128), BF16),
            jax.ShapeDtypeStruct((ROWS, height, 128), BF16),
        ),
        in_specs=[pl.BlockSpec(memory_space=pltpu.SMEM)] + [vmem] * len(operands),
        out_specs=(vmem, vmem),
        scratch_shapes=[pltpu.VMEM((2048, 256), BF16)],
        compiler_params=PARAMS,
        name=name,
    )(order, *operands)


def read_panels(gathered_ref, notes_ref, block, side, ids, weights):
    for source in range(ROWS):
        rows = slice(source * 128, (source + 1) * 128)
        side[rows, :128] = gathered_ref[source, :128]
        side[rows, 128:] = gathered_ref[source, 128:256]
        notes = notes_ref[source, 256:].astype(F32)
        high, low, weight = (notes[block * 3 + k : block * 3 + k + 1] for k in range(3))
        ids[:, rows] = (high * 64.0 + low).astype(jnp.int32)
        weights[:, rows] = weight


def panel_loads(side, ids, weights, first, tile, chunk):
    total = jnp.zeros((tile, 256), F32)
    for start in range(0, 2048, chunk):
        panels = slice(start, start + chunk)
        onehot = weighted_onehot(ids[:, panels], weights[:, panels].astype(BF16), first, tile)
        total += jnp.dot(onehot, side[panels], preferred_element_type=F32)
    return total


def first_loads_kernel(old_ref, gathered_ref, out_ref, side, ids, weights, *, tile, chunk):
    step = pl.program_id(0)

    @pl.when(step == 0)
    def _():
        read_panels(gathered_ref, gathered_ref, 0, side, ids, weights)

    total = panel_loads(side, ids, weights, step * tile, tile, chunk)
    for block in range(tile // 256):
        rows = slice(block * 256, (block + 1) * 256)
        out_ref[rows, :128] = total[rows, :128] + old_ref[block, :256].astype(F32)
        out_ref[rows, 128:] = total[rows, 128:] + old_ref[block, 256:].astype(F32)


def first_loads(old, gathered):
    tile = 1024
    return pl.pallas_call(
        functools.partial(first_loads_kernel, tile=tile, chunk=512),
        out_shape=jax.ShapeDtypeStruct((PATCHES, 256), F32),
        grid=(PATCHES // tile,),
        in_specs=[
            pl.BlockSpec((tile // 256, 512, 128), lambda step: (step, 0, 0)),
            pl.BlockSpec(gathered.shape, lambda step: (0, 0, 0)),
        ],
        out_specs=pl.BlockSpec((tile, 256), lambda step: (step, 0)),
        scratch_shapes=[
            pltpu.VMEM((2048, 256), BF16),
            pltpu.VMEM((1, 2048), jnp.int32),
            pltpu.VMEM((1, 2048), F32),
        ],
        compiler_params=PARAMS,
        name="first_loads",
    )(old, gathered)


def stress_kernel(order_ref, loads_ref, notes_ref, gathered_ref, *rest, tile, chunk):
    maps = rest[:COLS]
    out_ref, held, loads, side, ids, weights, sems = rest[COLS:]
    copies = [
        pltpu.make_async_copy(maps[k], held.at[k], sems.at[k]) for k in range(COLS)
    ]
    for copy in copies:
        copy.start()
    read_panels(gathered_ref, notes_ref, 1, side, ids, weights)
    for first in range(0, PATCHES, tile):
        rows = slice(first, first + tile)
        total = loads_ref[rows] + panel_loads(side, ids, weights, first, tile, chunk)
        loads[rows] = total.astype(BF16)
    for copy in copies:
        copy.wait()
    for first in range(0, 1024, 256):
        rows = slice(first, first + 256)
        real = jnp.zeros((256, 256), F32)
        imag = jnp.zeros((256, 256), F32)
        for k in range(COLS):
            part = loads[pl.ds(pl.multiple_of(order_ref[k] * 512, 512), 512)]
            real += jnp.dot(held[k, 0, rows], part, preferred_element_type=F32)
            imag += jnp.dot(held[k, 1, rows], part, preferred_element_type=F32)
        out_ref[0, rows] = (real[:, :128] - imag[:, 128:]).astype(BF16)
        out_ref[1, rows] = (real[:, 128:] + imag[:, :128]).astype(BF16)


def stress(order, loads, notes, gathered, maps):
    vmem = pl.BlockSpec(memory_space=pltpu.VMEM)
    return pl.pallas_call(
        functools.partial(stress_kernel, tile=1024, chunk=512),
        out_shape=jax.ShapeDtypeStruct((2, 1024, 128), BF16),
        in_specs=[pl.BlockSpec(memory_space=pltpu.SMEM)]
        + [vmem] * 3
        + [pl.BlockSpec(memory_space=pl.ANY)] * COLS,
        out_specs=vmem,
        scratch_shapes=[
            pltpu.VMEM((COLS, 2, 1024, 512), BF16),
            pltpu.VMEM((PATCHES, 256), BF16),
            pltpu.VMEM((2048, 256), BF16),
            pltpu.VMEM((1, 2048), jnp.int32),
            pltpu.VMEM((1, 2048), F32),
            pltpu.SemaphoreType.DMA((COLS,)),
        ],
        compiler_params=PARAMS,
        name="stress",
    )(order, loads, notes, gathered, *maps)


def from_chip(value, hop):
    pairs = [(i, (i // 2 + hop) % 4 * 2 + i % 2) for i in range(COLS)]
    return lax.ppermute(value, "col", pairs)


def other_core(value):
    return lax.ppermute(value, "col", [(i, i ^ 1) for i in range(COLS)])


def all_columns(matrix):
    own = jnp.stack([matrix] + [from_chip(matrix, hop) for hop in (1, 2, 3)])
    return own, other_core(own)


def to_rows(copies):
    return lax.all_to_all(copies, "row", 0, 0, tiled=True)


def on_device(
    rhs_first,
    rhs_last,
    inv_first,
    coupling,
    inv_last,
    earlier,
    patch_old,
    weight_old,
    patch_new,
    weight_new,
    stress_map,
):
    col = lax.axis_index("col")
    chips = [(col // 2 - hop) % 4 for hop in range(4)]
    core = col % 2
    order = jnp.stack(
        [chip * 2 + core for chip in chips] + [chip * 2 + 1 - core for chip in chips]
    ).astype(jnp.int32)

    first_all = all_columns(inv_first[None])
    later_all = all_columns(jnp.stack([coupling, inv_last]))
    own_core = [stress_map] + [from_chip(stress_map, hop) for hop in (1, 2, 3)]
    maps = own_core + [other_core(value) for value in own_core]

    rhs_all = to_rows(jnp.broadcast_to(rhs_first.reshape(1, 256, 128), (ROWS, 256, 128)))
    old_parts = to_rows(old_loads(patch_old[None], weight_old[None], earlier))

    notes = jnp.stack(
        [
            value
            for block in range(2)
            for value in (
                (patch_new[block] // 64).astype(BF16),
                (patch_new[block] % 64).astype(BF16),
                weight_new[block],
            )
        ]
    )
    notes = jnp.pad(notes, ((0, 10), (0, 0)))
    x_first, copies = rows_product("first_rows", order, first_all, 0, rhs_all, extra=notes)
    x_first_all = to_rows(copies)
    old_all = to_rows(sum_loads(old_parts))
    _, copies = rows_product("reduced_rows", order, later_all, 0, x_first_all, base=rhs_last)
    reduced_all = to_rows(copies)
    x_last, copies = rows_product("last_rows", order, later_all, 1, reduced_all)
    x_last_all = to_rows(copies)
    loads = first_loads(old_all, x_first_all)
    stress_rao = stress(order, loads, x_first_all, x_last_all, maps)
    return (jnp.stack([x_first, x_last]), stress_rao)


def solution(mesh):
    in_specs = (
        P(None, "row", "col"),
        P(None, "row", "col"),
        P(None, "row", "col"),
        P(None, "row", "col"),
        P(None, "row", "col"),
        P(None, "row", "col"),
        P("row"),
        P("row"),
        P(None, "row"),
        P(None, "row"),
        P(None, "row", "col"),
    )
    out_specs = (P(None, None, "row", "col"), P(None, "row", "col"))
    return jax.shard_map(
        on_device, mesh=mesh, in_specs=in_specs, out_specs=out_specs, check_vma=False
    )
```

```python
import functools

import jax
import jax.numpy as jnp
from jax import lax
from jax.experimental import pallas as pl
from jax.experimental.pallas import tpu as pltpu
from jax.sharding import PartitionSpec as P

PATCHES = 4096
ROWS = 16
COLS = 8
BF16 = jnp.bfloat16
F32 = jnp.float32
COST = pl.CostEstimate(flops=30_000_000_000, bytes_accessed=1000, transcendentals=0)
PARAMS = pltpu.CompilerParams(vmem_limit_bytes=20 * 2**20)


def weighted_onehot(ids, weights, first, count):
    patch = lax.broadcasted_iota(jnp.int32, (count, ids.shape[1]), 0)
    return jnp.where(patch == ids - first, weights, jnp.zeros((), BF16))


def old_loads_kernel(place_ref, ids_ref, weights_ref, earlier_ref, *rest, chunk):
    outs, side = rest[:4], rest[4]
    side[:, :128] = earlier_ref[0]
    side[:, 128:] = earlier_ref[1]
    ids = ids_ref[...]
    x, z = ids >> 10, (ids >> 8) & 3
    major = x + place_ref[2] * (z - x)
    minor = z + place_ref[2] * (x - z)
    labels = ((minor - place_ref[1]) & 3) * 1024 + major * 256 + (ids & 255)
    for k in range(4):
        total = jnp.zeros((1024, 256), F32)
        for start in range(0, side.shape[0], chunk):
            panels = slice(start, start + chunk)
            onehot = weighted_onehot(labels[:, panels], weights_ref[:, panels], k * 1024, 1024)
            total += jnp.dot(onehot, side[panels], preferred_element_type=F32)
        for block in range(4):
            rows = slice(block * 256, (block + 1) * 256)
            outs[k][block, :256] = total[rows, :128].astype(BF16)
            outs[k][block, 256:] = total[rows, 128:].astype(BF16)


def old_loads(place, ids, weights, earlier):
    panels = earlier.shape[1]
    vmem = pl.BlockSpec(memory_space=pltpu.VMEM)
    return pl.pallas_call(
        functools.partial(old_loads_kernel, chunk=512),
        out_shape=[jax.ShapeDtypeStruct((4, 512, 128), BF16)] * 4,
        in_specs=[pl.BlockSpec(memory_space=pltpu.SMEM)] + [vmem] * 3,
        out_specs=[vmem] * 4,
        scratch_shapes=[pltpu.VMEM((panels, 256), BF16)],
        compiler_params=PARAMS,
        name="old_loads",
    )(place, ids, weights, earlier)


def sum_loads_kernel(place_ref, *refs):
    parts, outs = refs[:4], refs[5:]
    for j in range(4):
        block = (place_ref[0] + j) % 4
        total = parts[0][block].astype(F32)
        for part in parts[1:]:
            total += part[block].astype(F32)
        outs[j][...] = total.astype(BF16)


def sum_loads(place, parts, tie):
    vmem = pl.BlockSpec(memory_space=pltpu.VMEM)
    return pl.pallas_call(
        sum_loads_kernel,
        out_shape=[jax.ShapeDtypeStruct((512, 128), BF16)] * 4,
        in_specs=[pl.BlockSpec(memory_space=pltpu.SMEM)]
        + [vmem] * 4
        + [pl.BlockSpec(memory_space=pl.ANY)],
        out_specs=[vmem] * 4,
        compiler_params=PARAMS,
        cost_estimate=COST,
        name="sum_loads",
    )(place, *parts, tie)


def add_loads_kernel(a_ref, b_ref, c_ref, d_ref, out_ref):
    total = a_ref[...].astype(F32) + b_ref[...].astype(F32)
    total += c_ref[...].astype(F32) + d_ref[...].astype(F32)
    out_ref[...] = total.astype(BF16)


def add_loads(parts):
    vmem = pl.BlockSpec(memory_space=pltpu.VMEM)
    return pl.pallas_call(
        add_loads_kernel,
        out_shape=jax.ShapeDtypeStruct((512, 128), BF16),
        in_specs=[vmem] * 4,
        out_specs=vmem,
        compiler_params=PARAMS,
        name="add_loads",
    )(*parts)


def pack_kernel(a_ref, b_ref, c_ref, d_ref, tie_ref, out_ref):
    for k, value_ref in enumerate((a_ref, b_ref, c_ref, d_ref)):
        out_ref[k] = value_ref[...]


def pack_loads(values, tie):
    vmem = pl.BlockSpec(memory_space=pltpu.VMEM)
    return pl.pallas_call(
        pack_kernel,
        out_shape=jax.ShapeDtypeStruct((4, *values[0].shape), BF16),
        in_specs=[vmem] * 4 + [pl.BlockSpec(memory_space=pl.ANY)],
        out_specs=vmem,
        compiler_params=PARAMS,
        cost_estimate=COST,
        name="pack_loads",
    )(*values, tie)


def send_copies(source, copies_ref, sems):
    copies = [
        pltpu.make_async_copy(source, copies_ref.at[k], sems.at[k]) for k in range(ROWS)
    ]
    for copy in copies:
        copy.start()
    for copy in copies:
        copy.wait()


def rows_kernel(factors_ref, gathered_ref, *rest, pick, base, extra, ties):
    rest = list(rest)
    base_ref = rest.pop(0) if base else None
    ids_ref, weights_ref = (rest.pop(0), rest.pop(0)) if extra else (None, None)
    out_ref, copies_ref, factor, side, send, notes, factor_sem, sems = rest[ties:]
    factor_copy = pltpu.make_async_copy(factors_ref.at[:, pick], factor, factor_sem)
    factor_copy.start()
    read_panels(gathered_ref, side)
    real = jnp.zeros((128, 256), F32)
    imag = jnp.zeros((128, 256), F32)
    factor_copy.wait()
    for block in range(COLS):
        part = side[block * 256 : (block + 1) * 256]
        real += jnp.dot(factor[block, 0], part, preferred_element_type=F32)
        imag += jnp.dot(factor[block, 1], part, preferred_element_type=F32)
    out_real = real[:, :128] - imag[:, 128:]
    out_imag = real[:, 128:] + imag[:, :128]
    if base:
        out_real = base_ref[0].astype(F32) - out_real
        out_imag = base_ref[1].astype(F32) - out_imag
    out_real = out_real.astype(BF16)
    out_imag = out_imag.astype(BF16)
    out_ref[0] = out_real
    out_ref[1] = out_imag
    send[:128] = out_real
    send[128:256] = out_imag
    if extra:
        notes[...] = jnp.zeros_like(notes)
        ids = ids_ref[...]
        notes[0:2] = (ids >> 6).astype(F32)
        notes[2:4] = (ids & 63).astype(F32)
        notes[4:6] = weights_ref[...].astype(F32)
        send[256:] = notes[...].astype(BF16)
    send_copies(send, copies_ref, sems)


def rows_product(name, factors, pick, gathered, base=None, extra=None, ties=()):
    vmem = pl.BlockSpec(memory_space=pltpu.VMEM)
    hbm = pl.BlockSpec(memory_space=pltpu.HBM)
    operands = [gathered]
    operands += [] if base is None else [base]
    operands += [] if extra is None else extra
    specs = [hbm] + [vmem] * len(operands)
    specs += [pl.BlockSpec(memory_space=pl.ANY)] * len(ties)
    height = 256 if extra is None else 272
    shapes = [jax.ShapeDtypeStruct((2, 128, 128), BF16), pltpu.HBM((ROWS, height, 128), BF16)]
    return pl.pallas_call(
        functools.partial(
            rows_kernel,
            pick=pick,
            base=base is not None,
            extra=extra is not None,
            ties=len(ties),
        ),
        out_shape=shapes,
        in_specs=specs,
        out_specs=[vmem, hbm],
        scratch_shapes=[
            pltpu.VMEM((COLS, 2, 128, 256), BF16),
            pltpu.VMEM((2048, 256), BF16),
            pltpu.VMEM((height, 128), BF16),
            pltpu.VMEM((16, 128), F32),
            pltpu.SemaphoreType.DMA,
            pltpu.SemaphoreType.DMA((ROWS,)),
        ],
        compiler_params=PARAMS,
        cost_estimate=COST,
        name=name,
    )(pltpu.with_memory_space_constraint(factors, pltpu.HBM), *operands, *ties)


def panel_loads(side, ids, weights, first, tile, chunk):
    total = jnp.zeros((tile, 256), F32)
    for start in range(0, 2048, chunk):
        panels = slice(start, start + chunk)
        onehot = weighted_onehot(ids[:, panels], weights[:, panels].astype(BF16), first, tile)
        total += jnp.dot(onehot, side[panels], preferred_element_type=F32)
    return total


def read_panels(gathered_ref, side):
    for source in range(ROWS):
        rows = slice(source * 128, (source + 1) * 128)
        side[rows, :128] = gathered_ref[source, :128]
        side[rows, 128:] = gathered_ref[source, 128:256]


def first_loads_kernel(place_ref, gathered_ref, *rest):
    old_refs = rest[:4]
    out_ref, ids_ref, weights_ref, side, ids, weights, old, total, old_sems, sems = rest[4:]
    old_copies = [
        pltpu.make_async_copy(old_refs[j], old.at[j], old_sems.at[j]) for j in range(4)
    ]
    for copy in old_copies:
        copy.start()
    read_panels(gathered_ref, side)
    for source in range(ROWS):
        rows = slice(source * 128, (source + 1) * 128)
        notes = gathered_ref[source, 256:].astype(F32)
        for block, (to_ids, to_weights) in enumerate(((ids, weights), (ids_ref, weights_ref))):
            high, low, weight = (notes[block + k : block + k + 1] for k in (0, 2, 4))
            to_ids[:, rows] = (high * 64.0 + low).astype(jnp.int32)
            to_weights[:, rows] = weight
    for first in range(0, PATCHES, 1024):
        total[first : first + 1024] = panel_loads(side, ids, weights, first, 1024, 512)
    copies = []
    for j in range(4):
        old_copies[j].wait()
        major = (place_ref[0] - j + 4) % 4
        for k in range(4):
            minor = (place_ref[1] - k + 4) % 4
            block = (major * 4 + minor) + place_ref[2] * 3 * (minor - major)
            rows = pl.ds(pl.multiple_of(block * 256, 256), 256)
            total[rows, :128] += old[j, k, :256].astype(F32)
            total[rows, 128:] += old[j, k, 256:].astype(F32)
            copies.append(
                pltpu.make_async_copy(total.at[rows], out_ref.at[rows], sems.at[j * 4 + k])
            )
            copies[-1].start()
    for copy in copies:
        copy.wait()


def first_loads(place, gathered, old):
    vmem = pl.BlockSpec(memory_space=pltpu.VMEM)
    hbm = pl.BlockSpec(memory_space=pltpu.HBM)
    return pl.pallas_call(
        first_loads_kernel,
        out_shape=(
            pltpu.HBM((PATCHES, 256), F32),
            jax.ShapeDtypeStruct((1, 2048), jnp.int32),
            jax.ShapeDtypeStruct((1, 2048), F32),
        ),
        in_specs=[pl.BlockSpec(memory_space=pltpu.SMEM), vmem]
        + [pl.BlockSpec(memory_space=pl.ANY)] * 4,
        out_specs=(hbm, vmem, vmem),
        scratch_shapes=[
            pltpu.VMEM((2048, 256), BF16),
            pltpu.VMEM((1, 2048), jnp.int32),
            pltpu.VMEM((1, 2048), F32),
            pltpu.VMEM((4, 4, 512, 128), BF16),
            pltpu.VMEM((PATCHES, 256), F32),
            pltpu.SemaphoreType.DMA((4,)),
            pltpu.SemaphoreType.DMA((ROWS,)),
        ],
        compiler_params=PARAMS,
        cost_estimate=COST,
        name="first_loads",
    )(place, gathered, *old)


def all_loads_kernel(
    ids, weights, gathered_ref, first_ref, maps_ref, out_ref, held_ref, side, first, first_sems, sems
):
    first_copies = []
    for part in range(4):
        rows = pl.ds(part * 1024, 1024)
        first_copies.append(
            pltpu.make_async_copy(first_ref.at[rows], first.at[rows], first_sems.at[part])
        )
    copies = [
        pltpu.make_async_copy(maps_ref.at[k], held_ref.at[k], sems.at[k]) for k in range(COLS)
    ]
    for copy in first_copies:
        copy.start()
    read_panels(gathered_ref, side)
    for part in range(4):
        rows = slice(part * 1024, (part + 1) * 1024)
        total = panel_loads(side, ids, weights, part * 1024, 1024, 512)
        first_copies[part].wait()
        out_ref[rows] = (first[rows] + total).astype(BF16)
        if part == 0:
            for copy in copies:
                copy.start()
    for copy in copies:
        copy.wait()


def all_loads(ids, weights, gathered, first, maps):
    vmem = pl.BlockSpec(memory_space=pltpu.VMEM)
    hbm = pl.BlockSpec(memory_space=pltpu.HBM)
    return pl.pallas_call(
        all_loads_kernel,
        out_shape=(pltpu.VMEM((PATCHES, 256), BF16), pltpu.VMEM(maps.shape, BF16)),
        in_specs=[vmem] * 3 + [hbm] * 2,
        out_specs=(vmem, vmem),
        scratch_shapes=[
            pltpu.VMEM((2048, 256), BF16),
            pltpu.VMEM((PATCHES, 256), F32),
            pltpu.SemaphoreType.DMA((4,)),
            pltpu.SemaphoreType.DMA((COLS,)),
        ],
        compiler_params=PARAMS,
        name="all_loads",
    )(
        ids,
        weights,
        gathered,
        pltpu.with_memory_space_constraint(first, pltpu.HBM),
        pltpu.with_memory_space_constraint(maps, pltpu.HBM),
    )


def stress_kernel(loads_ref, maps_ref, out_ref):
    for first in range(0, 1024, 512):
        rows = slice(first, first + 512)
        real = jnp.zeros((512, 256), F32)
        imag = jnp.zeros((512, 256), F32)
        for block in range(COLS):
            part = loads_ref[block * 512 : (block + 1) * 512]
            real += jnp.dot(maps_ref[block, 0, rows], part, preferred_element_type=F32)
            imag += jnp.dot(maps_ref[block, 1, rows], part, preferred_element_type=F32)
        out_ref[0, rows] = (real[:, :128] - imag[:, 128:]).astype(BF16)
        out_ref[1, rows] = (real[:, 128:] + imag[:, :128]).astype(BF16)


def stress(loads, maps):
    vmem = pl.BlockSpec(memory_space=pltpu.VMEM)
    return pl.pallas_call(
        stress_kernel,
        out_shape=jax.ShapeDtypeStruct((2, 1024, 128), BF16),
        in_specs=[vmem] * 2,
        out_specs=vmem,
        compiler_params=PARAMS,
        name="stress",
    )(
        pltpu.with_memory_space_constraint(loads, pltpu.VMEM),
        pltpu.with_memory_space_constraint(maps, pltpu.VMEM),
    )


def along_axis(value, hop, major):
    pairs = []
    for index in range(ROWS * COLS):
        x, z, rest = index // 32, index // 8 % 4, index % 8
        if major == (rest % 2 == 0):
            x = (x + hop) % 4
        else:
            z = (z + hop) % 4
        pairs.append((index, (x * 4 + z) * 8 + rest))
    return lax.ppermute(value, ("row", "col"), pairs)


def to_rows(copies):
    return lax.all_to_all(copies, "row", 0, 0, tiled=True)


def on_device(
    rhs_first,
    rhs_last,
    inv_first,
    coupling,
    inv_last,
    earlier,
    patch_old,
    weight_old,
    patch_new,
    weight_new,
    stress_map,
):
    row = lax.axis_index("row")
    col = lax.axis_index("col")
    core = col % 2
    x, z = row // 4, row % 4
    place = jnp.stack([x + core * (z - x), z + core * (x - z), core]).astype(jnp.int32)

    factors = lax.all_gather(jnp.stack([inv_first, coupling, inv_last]), "col")
    maps = lax.all_gather(stress_map, "col")
    rhs_all = to_rows(jnp.broadcast_to(rhs_first.reshape(1, 256, 128), (ROWS, 256, 128)))
    old = old_loads(place, patch_old[None], weight_old[None], earlier)
    x_first, copies = rows_product(
        "first_rows", factors, 0, rhs_all, extra=[patch_new, weight_new]
    )
    x_first_all = to_rows(copies)
    old = sum_loads(
        place, [old[0]] + [along_axis(old[hop], hop, False) for hop in (1, 2, 3)], x_first
    )
    old = add_loads([old[0]] + [along_axis(old[hop], hop, True) for hop in (1, 2, 3)])
    reduced, copies = rows_product(
        "reduced_rows", factors, 1, x_first_all, base=rhs_last, ties=(old,)
    )
    reduced_all = to_rows(copies)
    old = pack_loads([old] + [along_axis(old, hop, False) for hop in (1, 2, 3)], reduced)
    x_last, copies = rows_product("last_rows", factors, 2, reduced_all, ties=(old,))
    x_last_all = to_rows(copies)
    old = [old] + [along_axis(old, hop, True) for hop in (1, 2, 3)]
    loads, ids, weights = first_loads(place, x_first_all, old)
    stress_rao = stress(*all_loads(ids, weights, x_last_all, loads, maps))
    return (jnp.stack([x_first, x_last]), stress_rao)


def solution(mesh):
    in_specs = (
        P(None, "row", "col"),
        P(None, "row", "col"),
        P(None, "row", "col"),
        P(None, "row", "col"),
        P(None, "row", "col"),
        P(None, "row", "col"),
        P("row"),
        P("row"),
        P(None, "row"),
        P(None, "row"),
        P(None, "row", "col"),
    )
    out_specs = (P(None, None, "row", "col"), P(None, "row", "col"))
    return jax.shard_map(
        on_device, mesh=mesh, in_specs=in_specs, out_specs=out_specs, check_vma=False
    )
```

```python
import functools

import jax
import jax.numpy as jnp
from jax import lax
from jax.experimental import pallas as pl
from jax.experimental.pallas import tpu as pltpu
from jax.sharding import PartitionSpec as P

PATCHES = 4096
ROWS = 16
COLS = 8
BF16 = jnp.bfloat16
F32 = jnp.float32
COST = pl.CostEstimate(flops=30_000_000_000, bytes_accessed=1000, transcendentals=0)
PARAMS = pltpu.CompilerParams(vmem_limit_bytes=20 * 2**20)


def weighted_onehot(ids, weights, first, count):
    patch = lax.broadcasted_iota(jnp.int32, (count, ids.shape[1]), 0)
    return jnp.where(patch == ids - first, weights, jnp.zeros((), BF16))


def old_loads_kernel(place_ref, ids_ref, weights_ref, earlier_ref, *rest, chunk):
    outs, side = rest[:4], rest[4]
    side[:, :128] = earlier_ref[0]
    side[:, 128:] = earlier_ref[1]
    ids = ids_ref[...]
    x, z = ids >> 10, (ids >> 8) & 3
    major = x + place_ref[2] * (z - x)
    minor = z + place_ref[2] * (x - z)
    labels = ((minor - place_ref[1]) & 3) * 1024 + major * 256 + (ids & 255)
    for k in range(4):
        total = jnp.zeros((1024, 256), F32)
        for start in range(0, side.shape[0], chunk):
            panels = slice(start, start + chunk)
            onehot = weighted_onehot(labels[:, panels], weights_ref[:, panels], k * 1024, 1024)
            total += jnp.dot(onehot, side[panels], preferred_element_type=F32)
        for block in range(4):
            rows = slice(block * 256, (block + 1) * 256)
            outs[k][block, :256] = total[rows, :128].astype(BF16)
            outs[k][block, 256:] = total[rows, 128:].astype(BF16)


def old_loads(place, ids, weights, earlier):
    panels = earlier.shape[1]
    vmem = pl.BlockSpec(memory_space=pltpu.VMEM)
    return pl.pallas_call(
        functools.partial(old_loads_kernel, chunk=512),
        out_shape=[jax.ShapeDtypeStruct((4, 512, 128), BF16)] * 4,
        in_specs=[pl.BlockSpec(memory_space=pltpu.SMEM)] + [vmem] * 3,
        out_specs=[vmem] * 4,
        scratch_shapes=[pltpu.VMEM((panels, 256), BF16)],
        compiler_params=PARAMS,
        name="old_loads",
    )(place, ids, weights, earlier)


def sum_loads_kernel(a_ref, b_ref, c_ref, d_ref, tie_ref, out_ref):
    for block in range(4):
        total = a_ref[block].astype(F32) + b_ref[block].astype(F32)
        total += c_ref[block].astype(F32) + d_ref[block].astype(F32)
        out_ref[block] = total.astype(BF16)


def sum_loads(name, parts, tie):
    vmem = pl.BlockSpec(memory_space=pltpu.VMEM)
    return pl.pallas_call(
        sum_loads_kernel,
        out_shape=jax.ShapeDtypeStruct(parts[0].shape, BF16),
        in_specs=[vmem] * 4 + [pl.BlockSpec(memory_space=pl.ANY)],
        out_specs=vmem,
        compiler_params=PARAMS,
        cost_estimate=COST,
        name=name,
    )(*parts, tie)


def send_copies(source, copies_ref, sems):
    copies = [
        pltpu.make_async_copy(source, copies_ref.at[k], sems.at[k]) for k in range(ROWS)
    ]
    for copy in copies:
        copy.start()
    for copy in copies:
        copy.wait()


def rows_kernel(factors_ref, gathered_ref, *rest, pick, base, extra, ties):
    rest = list(rest)
    base_ref = rest.pop(0) if base else None
    ids_ref, weights_ref = (rest.pop(0), rest.pop(0)) if extra else (None, None)
    out_ref, copies_ref, factor, side, send, notes, factor_sem, sems = rest[ties:]
    factor_copy = pltpu.make_async_copy(factors_ref.at[:, pick], factor, factor_sem)
    factor_copy.start()
    read_panels(gathered_ref, side)
    total = jnp.zeros((256, 256), F32)
    factor_copy.wait()
    for block in range(COLS):
        part = side[block * 256 : (block + 1) * 256]
        left = factor[block].reshape(256, 256)
        total += jnp.dot(left, part, preferred_element_type=F32)
    out_real = total[:128, :128] - total[128:, 128:]
    out_imag = total[:128, 128:] + total[128:, :128]
    if base:
        out_real = base_ref[0].astype(F32) - out_real
        out_imag = base_ref[1].astype(F32) - out_imag
    out_real = out_real.astype(BF16)
    out_imag = out_imag.astype(BF16)
    out_ref[0] = out_real
    out_ref[1] = out_imag
    send[:128] = out_real
    send[128:256] = out_imag
    if extra:
        notes[...] = jnp.zeros_like(notes)
        ids = ids_ref[...]
        notes[0:2] = (ids >> 6).astype(F32)
        notes[2:4] = (ids & 63).astype(F32)
        notes[4:6] = weights_ref[...].astype(F32)
        send[256:] = notes[...].astype(BF16)
    send_copies(send, copies_ref, sems)


def rows_product(name, factors, pick, gathered, base=None, extra=None, ties=()):
    vmem = pl.BlockSpec(memory_space=pltpu.VMEM)
    hbm = pl.BlockSpec(memory_space=pltpu.HBM)
    operands = [gathered]
    operands += [] if base is None else [base]
    operands += [] if extra is None else extra
    specs = [hbm] + [vmem] * len(operands)
    specs += [pl.BlockSpec(memory_space=pl.ANY)] * len(ties)
    height = 256 if extra is None else 272
    shapes = [jax.ShapeDtypeStruct((2, 128, 128), BF16), pltpu.HBM((ROWS, height, 128), BF16)]
    return pl.pallas_call(
        functools.partial(
            rows_kernel,
            pick=pick,
            base=base is not None,
            extra=extra is not None,
            ties=len(ties),
        ),
        out_shape=shapes,
        in_specs=specs,
        out_specs=[vmem, hbm],
        scratch_shapes=[
            pltpu.VMEM((COLS, 2, 128, 256), BF16),
            pltpu.VMEM((2048, 256), BF16),
            pltpu.VMEM((height, 128), BF16),
            pltpu.VMEM((16, 128), F32),
            pltpu.SemaphoreType.DMA,
            pltpu.SemaphoreType.DMA((ROWS,)),
        ],
        compiler_params=PARAMS,
        cost_estimate=COST,
        name=name,
    )(pltpu.with_memory_space_constraint(factors, pltpu.HBM), *operands, *ties)


def panel_loads(side, ids, weights, first, tile, chunk):
    total = jnp.zeros((tile, 256), F32)
    for start in range(0, 2048, chunk):
        panels = slice(start, start + chunk)
        onehot = weighted_onehot(ids[:, panels], weights[:, panels].astype(BF16), first, tile)
        total += jnp.dot(onehot, side[panels], preferred_element_type=F32)
    return total


def read_panels(gathered_ref, side):
    for source in range(ROWS):
        rows = slice(source * 128, (source + 1) * 128)
        side[rows, :128] = gathered_ref[source, :128]
        side[rows, 128:] = gathered_ref[source, 128:256]


def first_loads_kernel(place_ref, gathered_ref, *rest):
    old_refs = rest[:4]
    out_ref, ids_ref, weights_ref, side, ids, weights, old, total, old_sems, sems = rest[4:]
    old_copies = [
        pltpu.make_async_copy(old_refs[j], old.at[j], old_sems.at[j]) for j in range(4)
    ]
    for copy in old_copies:
        copy.start()
    read_panels(gathered_ref, side)
    for source in range(ROWS):
        rows = slice(source * 128, (source + 1) * 128)
        notes = gathered_ref[source, 256:].astype(F32)
        for block, (to_ids, to_weights) in enumerate(((ids, weights), (ids_ref, weights_ref))):
            high, low, weight = (notes[block + k : block + k + 1] for k in (0, 2, 4))
            to_ids[:, rows] = (high * 64.0 + low).astype(jnp.int32)
            to_weights[:, rows] = weight
    for first in range(0, PATCHES, 1024):
        total[first : first + 1024] = panel_loads(side, ids, weights, first, 1024, 512)
    copies = []
    for j in range(4):
        old_copies[j].wait()
        minor = (place_ref[1] - j + 4) % 4
        for major in range(4):
            block = (major * 4 + minor) + place_ref[2] * 3 * (minor - major)
            rows = pl.ds(pl.multiple_of(block * 256, 256), 256)
            total[rows, :128] += old[j, major, :256].astype(F32)
            total[rows, 128:] += old[j, major, 256:].astype(F32)
            copies.append(
                pltpu.make_async_copy(total.at[rows], out_ref.at[rows], sems.at[j * 4 + major])
            )
            copies[-1].start()
    for copy in copies:
        copy.wait()


def first_loads(place, gathered, old):
    vmem = pl.BlockSpec(memory_space=pltpu.VMEM)
    hbm = pl.BlockSpec(memory_space=pltpu.HBM)
    return pl.pallas_call(
        first_loads_kernel,
        out_shape=(
            pltpu.HBM((PATCHES, 256), F32),
            jax.ShapeDtypeStruct((1, 2048), jnp.int32),
            jax.ShapeDtypeStruct((1, 2048), F32),
        ),
        in_specs=[pl.BlockSpec(memory_space=pltpu.SMEM), vmem]
        + [pl.BlockSpec(memory_space=pl.ANY)] * 4,
        out_specs=(hbm, vmem, vmem),
        scratch_shapes=[
            pltpu.VMEM((2048, 256), BF16),
            pltpu.VMEM((1, 2048), jnp.int32),
            pltpu.VMEM((1, 2048), F32),
            pltpu.VMEM((4, 4, 512, 128), BF16),
            pltpu.VMEM((PATCHES, 256), F32),
            pltpu.SemaphoreType.DMA((4,)),
            pltpu.SemaphoreType.DMA((ROWS,)),
        ],
        compiler_params=PARAMS,
        cost_estimate=COST,
        name="first_loads",
    )(place, gathered, *old)


def all_loads_kernel(ids, weights, gathered_ref, first_ref, out_ref, side, first, total, sem):
    copy = pltpu.make_async_copy(first_ref, first, sem)
    copy.start()
    read_panels(gathered_ref, side)
    for start in range(0, PATCHES, 1024):
        total[start : start + 1024] = panel_loads(side, ids, weights, start, 1024, 512)
    copy.wait()
    for start in range(0, PATCHES, 256):
        rows = slice(start, start + 256)
        out_ref[rows] = (first[rows] + total[rows]).astype(BF16)


def all_loads(ids, weights, gathered, first):
    vmem = pl.BlockSpec(memory_space=pltpu.VMEM)
    hbm = pl.BlockSpec(memory_space=pltpu.HBM)
    return pl.pallas_call(
        all_loads_kernel,
        out_shape=jax.ShapeDtypeStruct((PATCHES, 256), BF16),
        in_specs=[vmem] * 3 + [hbm],
        out_specs=vmem,
        scratch_shapes=[
            pltpu.VMEM((2048, 256), BF16),
            pltpu.VMEM((PATCHES, 256), F32),
            pltpu.VMEM((PATCHES, 256), F32),
            pltpu.SemaphoreType.DMA,
        ],
        compiler_params=PARAMS,
        name="all_loads",
    )(ids, weights, gathered, pltpu.with_memory_space_constraint(first, pltpu.HBM))


def stress_kernel(loads_ref, maps_ref, out_ref, held, sems):
    copies = []
    for step in range(4):
        rows = pl.ds(step * 256, 256)
        for block in range(COLS):
            source, target = maps_ref.at[block, :, rows], held.at[block, :, rows]
            copies.append(pltpu.make_async_copy(source, target, sems.at[step, block]))
            copies[-1].start()
    for step in range(4):
        for copy in copies[step * COLS : (step + 1) * COLS]:
            copy.wait()
        rows = slice(step * 256, (step + 1) * 256)
        real = jnp.zeros((256, 256), F32)
        imag = jnp.zeros((256, 256), F32)
        for block in range(COLS):
            part = loads_ref[block * 512 : (block + 1) * 512]
            real += jnp.dot(held[block, 0, rows], part, preferred_element_type=F32)
            imag += jnp.dot(held[block, 1, rows], part, preferred_element_type=F32)
        out_ref[0, rows] = (real[:, :128] - imag[:, 128:]).astype(BF16)
        out_ref[1, rows] = (real[:, 128:] + imag[:, :128]).astype(BF16)


def stress(loads, maps):
    vmem = pl.BlockSpec(memory_space=pltpu.VMEM)
    return pl.pallas_call(
        stress_kernel,
        out_shape=jax.ShapeDtypeStruct((2, 1024, 128), BF16),
        in_specs=[vmem, pl.BlockSpec(memory_space=pltpu.HBM)],
        out_specs=vmem,
        scratch_shapes=[
            pltpu.VMEM((COLS, 2, 1024, 512), BF16),
            pltpu.SemaphoreType.DMA((4, COLS)),
        ],
        compiler_params=pltpu.CompilerParams(vmem_limit_bytes=32 * 2**20),
        name="stress",
    )(loads, pltpu.with_memory_space_constraint(maps, pltpu.HBM))


def along_axis(value, hop, major):
    pairs = []
    for index in range(ROWS * COLS):
        x, z, rest = index // 32, index // 8 % 4, index % 8
        if major == (rest % 2 == 0):
            x = (x + hop) % 4
        else:
            z = (z + hop) % 4
        pairs.append((index, (x * 4 + z) * 8 + rest))
    return lax.ppermute(value, ("row", "col"), pairs)


def to_rows(copies):
    return lax.all_to_all(copies, "row", 0, 0, tiled=True)


def on_device(
    rhs_first,
    rhs_last,
    inv_first,
    coupling,
    inv_last,
    earlier,
    patch_old,
    weight_old,
    patch_new,
    weight_new,
    stress_map,
):
    row = lax.axis_index("row")
    col = lax.axis_index("col")
    core = col % 2
    x, z = row // 4, row % 4
    place = jnp.stack([x + core * (z - x), z + core * (x - z), core]).astype(jnp.int32)


    factors = lax.all_gather(jnp.stack([inv_first, coupling, inv_last]), "col")
    maps = lax.all_gather(stress_map, "col")
    rhs_all = to_rows(jnp.broadcast_to(rhs_first.reshape(1, 256, 128), (ROWS, 256, 128)))
    old = old_loads(place, patch_old[None], weight_old[None], earlier)
    x_first, copies = rows_product(
        "first_rows", factors, 0, rhs_all, extra=[patch_new, weight_new], ties=(old[0],)
    )
    x_first_all = to_rows(copies)
    old = [old[0]] + [along_axis(old[hop], hop, False) for hop in (1, 2, 3)]
    old = sum_loads("sum_minor", old, x_first)
    reduced, copies = rows_product(
        "reduced_rows", factors, 1, x_first_all, base=rhs_last, ties=(old,)
    )
    reduced_all = to_rows(copies)
    old = [old] + [along_axis(old, hop, True) for hop in (1, 2, 3)]
    old = sum_loads("sum_major", old, reduced)
    x_last, copies = rows_product("last_rows", factors, 2, reduced_all, ties=(old,))
    x_last_all = to_rows(copies)
    old = [old] + [along_axis(old, hop, False) for hop in (1, 2, 3)]
    loads, ids, weights = first_loads(place, x_first_all, old)
    stress_rao = stress(all_loads(ids, weights, x_last_all, loads), maps)
    return (jnp.stack([x_first, x_last]), stress_rao)


def solution(mesh):
    in_specs = (
        P(None, "row", "col"),
        P(None, "row", "col"),
        P(None, "row", "col"),
        P(None, "row", "col"),
        P(None, "row", "col"),
        P(None, "row", "col"),
        P("row"),
        P("row"),
        P(None, "row"),
        P(None, "row"),
        P(None, "row", "col"),
    )
    out_specs = (P(None, None, "row", "col"), P(None, "row", "col"))
    return jax.shard_map(
        on_device, mesh=mesh, in_specs=in_specs, out_specs=out_specs, check_vma=False
    )
```

```python
import functools

import jax
import jax.numpy as jnp
from jax import lax
from jax.experimental import pallas as pl
from jax.experimental.pallas import tpu as pltpu
from jax.sharding import PartitionSpec as P

PATCHES = 4096
ROWS = 16
COLS = 8
BF16 = jnp.bfloat16
F32 = jnp.float32
COST = pl.CostEstimate(flops=30_000_000_000, bytes_accessed=1000, transcendentals=0)
SHORT = pl.CostEstimate(flops=6_000_000_000, bytes_accessed=1000, transcendentals=0)
BRIEF = pl.CostEstimate(flops=1_000_000_000, bytes_accessed=1000, transcendentals=0)
PARAMS = pltpu.CompilerParams(vmem_limit_bytes=20 * 2**20)


def weighted_onehot(ids, weights, first, count):
    patch = lax.broadcasted_iota(jnp.int32, (count, ids.shape[1]), 0)
    return jnp.where(patch == ids - first, weights, jnp.zeros((), BF16))


def old_loads_kernel(place_ref, ids_ref, weights_ref, earlier_ref, *rest, chunk):
    outs, side = rest[:4], rest[4]
    side[:, :128] = earlier_ref[0]
    side[:, 128:] = earlier_ref[1]
    ids = ids_ref[...]
    x, z = ids >> 10, (ids >> 8) & 3
    major = x + place_ref[2] * (z - x)
    minor = z + place_ref[2] * (x - z)
    labels = ((minor - place_ref[1]) & 3) * 1024 + major * 256 + (ids & 255)
    for k in range(4):
        total = jnp.zeros((1024, 256), F32)
        for start in range(0, side.shape[0], chunk):
            panels = slice(start, start + chunk)
            onehot = weighted_onehot(labels[:, panels], weights_ref[:, panels], k * 1024, 1024)
            total += jnp.dot(onehot, side[panels], preferred_element_type=F32)
        for block in range(4):
            rows = slice(block * 256, (block + 1) * 256)
            outs[k][block, :256] = total[rows, :128].astype(BF16)
            outs[k][block, 256:] = total[rows, 128:].astype(BF16)


def old_loads(place, ids, weights, earlier):
    panels = earlier.shape[1]
    vmem = pl.BlockSpec(memory_space=pltpu.VMEM)
    return pl.pallas_call(
        functools.partial(old_loads_kernel, chunk=512),
        out_shape=[jax.ShapeDtypeStruct((4, 512, 128), BF16)] * 4,
        in_specs=[pl.BlockSpec(memory_space=pltpu.SMEM)] + [vmem] * 3,
        out_specs=[vmem] * 4,
        scratch_shapes=[pltpu.VMEM((panels, 256), BF16)],
        compiler_params=PARAMS,
        name="old_loads",
    )(place, ids, weights, earlier)


def sum_loads_kernel(a_ref, b_ref, c_ref, d_ref, tie_ref, out_ref):
    for block in range(4):
        total = a_ref[block].astype(F32) + b_ref[block].astype(F32)
        total += c_ref[block].astype(F32) + d_ref[block].astype(F32)
        out_ref[block] = total.astype(BF16)


def sum_loads(name, parts, tie):
    vmem = pl.BlockSpec(memory_space=pltpu.VMEM)
    return pl.pallas_call(
        sum_loads_kernel,
        out_shape=jax.ShapeDtypeStruct(parts[0].shape, BF16),
        in_specs=[vmem] * 4 + [pl.BlockSpec(memory_space=pl.ANY)],
        out_specs=vmem,
        compiler_params=PARAMS,
        cost_estimate=COST,
        name=name,
    )(*parts, tie)


def pack_factors_kernel(a_ref, b_ref, c_ref, d_ref, tie_ref, *outs):
    for k, value_ref in enumerate((a_ref, b_ref, c_ref, d_ref)):
        outs[k // 2][k % 2] = value_ref[0]
        outs[2][k] = value_ref[1]
        outs[3][k] = value_ref[2]


def pack_factors(values, tie):
    vmem = pl.BlockSpec(memory_space=pltpu.VMEM)
    return pl.pallas_call(
        pack_factors_kernel,
        out_shape=[
            jax.ShapeDtypeStruct((count, *values[0].shape[1:]), BF16) for count in (2, 2, 4, 4)
        ],
        in_specs=[vmem] * 4 + [pl.BlockSpec(memory_space=pl.ANY)],
        out_specs=[vmem] * 4,
        compiler_params=PARAMS,
        cost_estimate=SHORT,
        name="pack_factors",
    )(*values, tie)


def send_copies(source, copies_ref, sems):
    copies = [
        pltpu.make_async_copy(source, copies_ref.at[k], sems.at[k]) for k in range(ROWS)
    ]
    for copy in copies:
        copy.start()
    for copy in copies:
        copy.wait()


def rows_kernel(*rest, parts, base, extra, ties):
    factor_refs, gathered_ref, rest = rest[:parts], rest[parts], list(rest[parts + 1 :])
    base_ref = rest.pop(0) if base else None
    ids_ref, weights_ref = (rest.pop(0), rest.pop(0)) if extra else (None, None)
    out_ref, copies_ref, factor, side, send, notes, factor_sems, sems = rest[ties:]
    size = COLS // parts
    factor_copies = [
        pltpu.make_async_copy(part_ref, factor.at[pl.ds(k * size, size)], factor_sems.at[k])
        for k, part_ref in enumerate(factor_refs)
    ]
    for copy in factor_copies:
        copy.start()
    col = lax.axis_index("col")
    core = col % 2
    for block in range(COLS):
        chip = (col // 2 + 4 - block % 4) % 4
        column = chip * 2 + (core if block < 4 else 1 - core)
        for half in range(2):
            source = column * 2 + half
            rows = slice(block * 256 + half * 128, block * 256 + (half + 1) * 128)
            side[rows, :128] = gathered_ref[source, :128]
            side[rows, 128:] = gathered_ref[source, 128:256]
    total = jnp.zeros((256, 256), F32)
    for copy in factor_copies:
        copy.wait()
    for block in range(COLS):
        part = side[block * 256 : (block + 1) * 256]
        left = factor[block].reshape(256, 256)
        total += jnp.dot(left, part, preferred_element_type=F32)
    out_real = total[:128, :128] - total[128:, 128:]
    out_imag = total[:128, 128:] + total[128:, :128]
    if base:
        out_real = base_ref[0].astype(F32) - out_real
        out_imag = base_ref[1].astype(F32) - out_imag
    out_real = out_real.astype(BF16)
    out_imag = out_imag.astype(BF16)
    out_ref[0] = out_real
    out_ref[1] = out_imag
    send[:128] = out_real
    send[128:256] = out_imag
    if extra:
        notes[...] = jnp.zeros_like(notes)
        ids = ids_ref[...]
        notes[0:2] = (ids >> 6).astype(F32)
        notes[2:4] = (ids & 63).astype(F32)
        notes[4:6] = weights_ref[...].astype(F32)
        send[256:] = notes[...].astype(BF16)
    send_copies(send, copies_ref, sems)


def rows_product(name, factors, gathered, base=None, extra=None, ties=(), cost=COST):
    vmem = pl.BlockSpec(memory_space=pltpu.VMEM)
    hbm = pl.BlockSpec(memory_space=pltpu.HBM)
    operands = [gathered]
    operands += [] if base is None else [base]
    operands += [] if extra is None else extra
    specs = [hbm] * len(factors) + [vmem] * len(operands)
    specs += [pl.BlockSpec(memory_space=pl.ANY)] * len(ties)
    height = 256 if extra is None else 272
    shapes = [jax.ShapeDtypeStruct((2, 128, 128), BF16), pltpu.HBM((ROWS, height, 128), BF16)]
    return pl.pallas_call(
        functools.partial(
            rows_kernel,
            parts=len(factors),
            base=base is not None,
            extra=extra is not None,
            ties=len(ties),
        ),
        out_shape=shapes,
        in_specs=specs,
        out_specs=[vmem, hbm],
        scratch_shapes=[
            pltpu.VMEM((COLS, 2, 128, 256), BF16),
            pltpu.VMEM((2048, 256), BF16),
            pltpu.VMEM((height, 128), BF16),
            pltpu.VMEM((16, 128), F32),
            pltpu.SemaphoreType.DMA((4,)),
            pltpu.SemaphoreType.DMA((ROWS,)),
        ],
        compiler_params=PARAMS,
        cost_estimate=cost,
        name=name,
    )(
        *[pltpu.with_memory_space_constraint(part, pltpu.HBM) for part in factors],
        *operands,
        *ties,
    )


def panel_loads(side, ids, weights, first, tile, chunk):
    total = jnp.zeros((tile, 256), F32)
    for start in range(0, 2048, chunk):
        panels = slice(start, start + chunk)
        onehot = weighted_onehot(ids[:, panels], weights[:, panels].astype(BF16), first, tile)
        total += jnp.dot(onehot, side[panels], preferred_element_type=F32)
    return total


def read_panels(gathered_ref, side):
    for source in range(ROWS):
        rows = slice(source * 128, (source + 1) * 128)
        side[rows, :128] = gathered_ref[source, :128]
        side[rows, 128:] = gathered_ref[source, 128:256]


def first_loads_kernel(place_ref, gathered_ref, *rest):
    old_refs = rest[:4]
    out_ref, ids_ref, weights_ref, side, ids, weights, old, total, old_sems, sems = rest[4:]
    old_copies = [
        pltpu.make_async_copy(old_refs[j], old.at[j], old_sems.at[j]) for j in range(4)
    ]
    for copy in old_copies:
        copy.start()
    read_panels(gathered_ref, side)
    for source in range(ROWS):
        rows = slice(source * 128, (source + 1) * 128)
        notes = gathered_ref[source, 256:].astype(F32)
        for block, (to_ids, to_weights) in enumerate(((ids, weights), (ids_ref, weights_ref))):
            high, low, weight = (notes[block + k : block + k + 1] for k in (0, 2, 4))
            to_ids[:, rows] = (high * 64.0 + low).astype(jnp.int32)
            to_weights[:, rows] = weight
    for first in range(0, PATCHES, 1024):
        total[first : first + 1024] = panel_loads(side, ids, weights, first, 1024, 512)
    copies = []
    for j in range(4):
        old_copies[j].wait()
        minor = (place_ref[1] + j) % 4
        for major in range(4):
            block = (major * 4 + minor) + place_ref[2] * 3 * (minor - major)
            rows = pl.ds(pl.multiple_of(block * 256, 256), 256)
            total[rows, :128] += old[j, major, :256].astype(F32)
            total[rows, 128:] += old[j, major, 256:].astype(F32)
            copies.append(
                pltpu.make_async_copy(total.at[rows], out_ref.at[rows], sems.at[j * 4 + major])
            )
            copies[-1].start()
    for copy in copies:
        copy.wait()


def first_loads(place, gathered, old):
    vmem = pl.BlockSpec(memory_space=pltpu.VMEM)
    hbm = pl.BlockSpec(memory_space=pltpu.HBM)
    return pl.pallas_call(
        first_loads_kernel,
        out_shape=(
            pltpu.HBM((PATCHES, 256), F32),
            jax.ShapeDtypeStruct((1, 2048), jnp.int32),
            jax.ShapeDtypeStruct((1, 2048), F32),
        ),
        in_specs=[pl.BlockSpec(memory_space=pltpu.SMEM), vmem]
        + [pl.BlockSpec(memory_space=pl.ANY)] * 4,
        out_specs=(hbm, vmem, vmem),
        scratch_shapes=[
            pltpu.VMEM((2048, 256), BF16),
            pltpu.VMEM((1, 2048), jnp.int32),
            pltpu.VMEM((1, 2048), F32),
            pltpu.VMEM((4, 4, 512, 128), BF16),
            pltpu.VMEM((PATCHES, 256), F32),
            pltpu.SemaphoreType.DMA((4,)),
            pltpu.SemaphoreType.DMA((ROWS,)),
        ],
        compiler_params=PARAMS,
        cost_estimate=COST,
        name="first_loads",
    )(place, gathered, *old)


def all_loads_kernel(
    ids, weights, gathered_ref, first_ref, maps_ref, out_ref, held_ref, side, first, total, sem, sems
):
    first_copy = pltpu.make_async_copy(first_ref, first, sem)
    first_copy.start()
    copies = [
        pltpu.make_async_copy(maps_ref.at[k], held_ref.at[k], sems.at[k]) for k in range(COLS)
    ]
    for copy in copies:
        copy.start()
    read_panels(gathered_ref, side)
    for start in range(0, PATCHES, 1024):
        total[start : start + 1024] = panel_loads(side, ids, weights, start, 1024, 512)
    first_copy.wait()
    for start in range(0, PATCHES, 256):
        rows = slice(start, start + 256)
        out_ref[rows] = (first[rows] + total[rows]).astype(BF16)
    for copy in copies:
        copy.wait()


def all_loads(ids, weights, gathered, first, maps):
    vmem = pl.BlockSpec(memory_space=pltpu.VMEM)
    hbm = pl.BlockSpec(memory_space=pltpu.HBM)
    return pl.pallas_call(
        all_loads_kernel,
        out_shape=(pltpu.VMEM((PATCHES, 256), BF16), pltpu.VMEM(maps.shape, BF16)),
        in_specs=[vmem] * 3 + [hbm] * 2,
        out_specs=(vmem, vmem),
        scratch_shapes=[
            pltpu.VMEM((2048, 256), BF16),
            pltpu.VMEM((PATCHES, 256), F32),
            pltpu.VMEM((PATCHES, 256), F32),
            pltpu.SemaphoreType.DMA,
            pltpu.SemaphoreType.DMA((COLS,)),
        ],
        compiler_params=PARAMS,
        name="all_loads",
    )(
        ids,
        weights,
        gathered,
        pltpu.with_memory_space_constraint(first, pltpu.HBM),
        pltpu.with_memory_space_constraint(maps, pltpu.HBM),
    )


def stress_kernel(loads_ref, maps_ref, out_ref):
    for first in range(0, 1024, 512):
        rows = slice(first, first + 512)
        real = jnp.zeros((512, 256), F32)
        imag = jnp.zeros((512, 256), F32)
        for block in range(COLS):
            part = loads_ref[block * 512 : (block + 1) * 512]
            real += jnp.dot(maps_ref[block, 0, rows], part, preferred_element_type=F32)
            imag += jnp.dot(maps_ref[block, 1, rows], part, preferred_element_type=F32)
        out_ref[0, rows] = (real[:, :128] - imag[:, 128:]).astype(BF16)
        out_ref[1, rows] = (real[:, 128:] + imag[:, :128]).astype(BF16)


def stress(loads, maps):
    vmem = pl.BlockSpec(memory_space=pltpu.VMEM)
    return pl.pallas_call(
        stress_kernel,
        out_shape=jax.ShapeDtypeStruct((2, 1024, 128), BF16),
        in_specs=[vmem] * 2,
        out_specs=vmem,
        compiler_params=PARAMS,
        name="stress",
    )(
        pltpu.with_memory_space_constraint(loads, pltpu.VMEM),
        pltpu.with_memory_space_constraint(maps, pltpu.VMEM),
    )


def along_y(value, hop):
    pairs = [(i, (i // 2 + hop) % 4 * 2 + i % 2) for i in range(COLS)]
    return lax.ppermute(value, "col", pairs)


def other_core(value):
    return lax.ppermute(value, "col", [(i, i ^ 1) for i in range(COLS)])


def along_axis(value, hop, major):
    pairs = []
    for index in range(ROWS * COLS):
        x, z, rest = index // 32, index // 8 % 4, index % 8
        if major == (rest % 2 == 1):
            x = (x + hop) % 4
        else:
            z = (z + hop) % 4
        pairs.append((index, (x * 4 + z) * 8 + rest))
    return lax.ppermute(value, ("row", "col"), pairs)


def to_rows(copies):
    return lax.all_to_all(copies, "row", 0, 0, tiled=True)


def on_device(
    rhs_first,
    rhs_last,
    inv_first,
    coupling,
    inv_last,
    earlier,
    patch_old,
    weight_old,
    patch_new,
    weight_new,
    stress_map,
):
    row = lax.axis_index("row")
    col = lax.axis_index("col")
    core = col % 2
    x, z = row // 4, row % 4
    swap = 1 - core
    place = jnp.stack([x + swap * (z - x), z + swap * (x - z), swap]).astype(jnp.int32)


    rhs_all = to_rows(jnp.broadcast_to(rhs_first.reshape(1, 256, 128), (ROWS, 256, 128)))
    maps = lax.all_gather(stress_map, "col")
    factors = jnp.stack([inv_first, coupling, inv_last])
    factors = [factors] + [along_y(factors, hop) for hop in (1, 2, 3)]
    old = old_loads(place, patch_old[None], weight_old[None], earlier)
    own = list(pack_factors(factors, old[0]))
    other = [other_core(value) for value in own]
    factors = [own[:2] + other[:2], [own[2], other[2]], [own[3], other[3]]]
    x_first, copies = rows_product(
        "first_rows", factors[0], rhs_all, extra=[patch_new, weight_new], cost=BRIEF
    )
    x_first_all = to_rows(copies)
    old = [old[0]] + [along_axis(old[hop], hop, False) for hop in (1, 2, 3)]
    old = sum_loads("sum_minor", old, x_first)
    reduced, copies = rows_product(
        "reduced_rows", factors[1], x_first_all, base=rhs_last, ties=(old,)
    )
    reduced_all = to_rows(copies)
    old = [old] + [along_axis(old, hop, True) for hop in (3, 2, 1)]
    old = sum_loads("sum_major", old, reduced)
    x_last, copies = rows_product("last_rows", factors[2], reduced_all, ties=(old,))
    x_last_all = to_rows(copies)
    old = [old] + [along_axis(old, hop, False) for hop in (3, 2, 1)]
    loads, ids, weights = first_loads(place, x_first_all, old)
    stress_rao = stress(*all_loads(ids, weights, x_last_all, loads, maps))
    return (jnp.stack([x_first, x_last]), stress_rao)


def solution(mesh):
    in_specs = (
        P(None, "row", "col"),
        P(None, "row", "col"),
        P(None, "row", "col"),
        P(None, "row", "col"),
        P(None, "row", "col"),
        P(None, "row", "col"),
        P("row"),
        P("row"),
        P(None, "row"),
        P(None, "row"),
        P(None, "row", "col"),
    )
    out_specs = (P(None, None, "row", "col"), P(None, "row", "col"))
    return jax.shard_map(
        on_device, mesh=mesh, in_specs=in_specs, out_specs=out_specs, check_vma=False
    )
```

```python
import functools

import jax
import jax.numpy as jnp
from jax import lax
from jax.experimental import pallas as pl
from jax.experimental.pallas import tpu as pltpu
from jax.sharding import PartitionSpec as P

PATCHES = 4096
ROWS = 16
COLS = 8
BF16 = jnp.bfloat16
F32 = jnp.float32
COST = pl.CostEstimate(flops=30_000_000_000, bytes_accessed=1000, transcendentals=0)
SHORT = pl.CostEstimate(flops=6_000_000_000, bytes_accessed=1000, transcendentals=0)
BRIEF = pl.CostEstimate(flops=1_000_000_000, bytes_accessed=1000, transcendentals=0)
PARAMS = pltpu.CompilerParams(vmem_limit_bytes=20 * 2**20)


def weighted_onehot(ids, weights, first, count):
    patch = lax.broadcasted_iota(jnp.int32, (count, ids.shape[1]), 0)
    return jnp.where(patch == ids - first, weights, jnp.zeros((), BF16))


def minor_place():
    row = lax.axis_index("row")
    x, z = row // 4, row % 4
    swap = 1 - lax.axis_index("col") % 2
    return z + swap * (x - z), swap


def old_loads_kernel(ids_ref, weights_ref, earlier_ref, *rest, chunk):
    outs, side = rest[:4], rest[4]
    side[:, :128] = earlier_ref[0]
    side[:, 128:] = earlier_ref[1]
    ids = ids_ref[...]
    x, z = ids >> 10, (ids >> 8) & 3
    place, swap = minor_place()
    major = x + swap * (z - x)
    minor = z + swap * (x - z)
    labels = ((minor - place) & 3) * 1024 + major * 256 + (ids & 255)
    for k in range(4):
        total = jnp.zeros((1024, 256), F32)
        for start in range(0, side.shape[0], chunk):
            panels = slice(start, start + chunk)
            onehot = weighted_onehot(labels[:, panels], weights_ref[:, panels], k * 1024, 1024)
            total += jnp.dot(onehot, side[panels], preferred_element_type=F32)
        for block in range(4):
            rows = slice(block * 256, (block + 1) * 256)
            outs[k][block, :256] = total[rows, :128].astype(BF16)
            outs[k][block, 256:] = total[rows, 128:].astype(BF16)


def old_loads(ids, weights, earlier):
    panels = earlier.shape[1]
    vmem = pl.BlockSpec(memory_space=pltpu.VMEM)
    return pl.pallas_call(
        functools.partial(old_loads_kernel, chunk=512),
        out_shape=[jax.ShapeDtypeStruct((4, 512, 128), BF16)] * 4,
        in_specs=[vmem] * 3,
        out_specs=[vmem] * 4,
        scratch_shapes=[pltpu.VMEM((panels, 256), BF16)],
        compiler_params=PARAMS,
        name="old_loads",
    )(ids, weights, earlier)


def sum_loads_kernel(a_ref, b_ref, c_ref, d_ref, tie_ref, out_ref):
    for block in range(4):
        total = a_ref[block].astype(F32) + b_ref[block].astype(F32)
        total += c_ref[block].astype(F32) + d_ref[block].astype(F32)
        out_ref[block] = total.astype(BF16)


def sum_loads(name, parts, tie):
    vmem = pl.BlockSpec(memory_space=pltpu.VMEM)
    return pl.pallas_call(
        sum_loads_kernel,
        out_shape=jax.ShapeDtypeStruct(parts[0].shape, BF16),
        in_specs=[vmem] * 4 + [pl.BlockSpec(memory_space=pl.ANY)],
        out_specs=vmem,
        compiler_params=PARAMS,
        cost_estimate=COST,
        name=name,
    )(*parts, tie)


def pack_factors_kernel(*refs):
    values, outs, sems = refs[:4], refs[5:9], refs[9]
    copies = []
    for k in range(4):
        targets = (outs[k // 2].at[k % 2], outs[2].at[k], outs[3].at[k])
        for m in range(3):
            copies.append(pltpu.make_async_copy(values[k].at[m], targets[m], sems.at[k, m]))
            copies[-1].start()
    for copy in copies:
        copy.wait()


def pack_factors(values, tie):
    vmem = pl.BlockSpec(memory_space=pltpu.VMEM)
    return pl.pallas_call(
        pack_factors_kernel,
        out_shape=[
            jax.ShapeDtypeStruct((count, *values[0].shape[1:]), BF16) for count in (2, 2, 4, 4)
        ],
        in_specs=[pl.BlockSpec(memory_space=pl.ANY)] * 5,
        out_specs=[vmem] * 4,
        scratch_shapes=[pltpu.SemaphoreType.DMA((4, 3))],
        compiler_params=PARAMS,
        cost_estimate=SHORT,
        name="pack_factors",
    )(
        values[0],
        *[pltpu.with_memory_space_constraint(value, pltpu.HBM) for value in values[1:]],
        tie,
    )


def send_copies(source, copies_ref, sems):
    copies = [
        pltpu.make_async_copy(source, copies_ref.at[k], sems.at[k]) for k in range(ROWS)
    ]
    for copy in copies:
        copy.start()
    for copy in copies:
        copy.wait()


def rows_kernel(*rest, parts, base, extra, ties):
    factor_refs, gathered_ref, rest = rest[:parts], rest[parts], list(rest[parts + 1 :])
    base_ref = rest.pop(0) if base else None
    ids_ref, weights_ref = (rest.pop(0), rest.pop(0)) if extra else (None, None)
    out_ref, copies_ref, factor, side, send, notes, factor_sems, sems = rest[ties:]
    size = COLS // parts
    factor_copies = [
        pltpu.make_async_copy(part_ref, factor.at[pl.ds(k * size, size)], factor_sems.at[k])
        for k, part_ref in enumerate(factor_refs)
    ]
    for copy in factor_copies:
        copy.start()
    col = lax.axis_index("col")
    core = col % 2
    for block in range(COLS):
        chip = (col // 2 + 4 - block % 4) % 4
        column = chip * 2 + (core if block < 4 else 1 - core)
        for half in range(2):
            source = column * 2 + half
            rows = slice(block * 256 + half * 128, block * 256 + (half + 1) * 128)
            side[rows, :128] = gathered_ref[source, :128]
            side[rows, 128:] = gathered_ref[source, 128:256]
    total = jnp.zeros((256, 256), F32)
    for copy in factor_copies:
        copy.wait()
    for block in range(COLS):
        part = side[block * 256 : (block + 1) * 256]
        left = factor[block].reshape(256, 256)
        total += jnp.dot(left, part, preferred_element_type=F32)
    out_real = total[:128, :128] - total[128:, 128:]
    out_imag = total[:128, 128:] + total[128:, :128]
    if base:
        out_real = base_ref[0].astype(F32) - out_real
        out_imag = base_ref[1].astype(F32) - out_imag
    out_real = out_real.astype(BF16)
    out_imag = out_imag.astype(BF16)
    out_ref[0] = out_real
    out_ref[1] = out_imag
    send[:128] = out_real
    send[128:256] = out_imag
    if extra:
        notes[...] = jnp.zeros_like(notes)
        ids = ids_ref[...]
        notes[0:2] = (ids >> 6).astype(F32)
        notes[2:4] = (ids & 63).astype(F32)
        notes[4:6] = weights_ref[...].astype(F32)
        send[256:] = notes[...].astype(BF16)
    send_copies(send, copies_ref, sems)


def rows_product(name, factors, gathered, base=None, extra=None, ties=(), cost=COST):
    vmem = pl.BlockSpec(memory_space=pltpu.VMEM)
    hbm = pl.BlockSpec(memory_space=pltpu.HBM)
    operands = [gathered]
    operands += [] if base is None else [base]
    operands += [] if extra is None else extra
    specs = [pl.BlockSpec(memory_space=pl.ANY)] * len(factors) + [vmem] * len(operands)
    specs += [pl.BlockSpec(memory_space=pl.ANY)] * len(ties)
    height = 256 if extra is None else 272
    shapes = [jax.ShapeDtypeStruct((2, 128, 128), BF16), pltpu.HBM((ROWS, height, 128), BF16)]
    return pl.pallas_call(
        functools.partial(
            rows_kernel,
            parts=len(factors),
            base=base is not None,
            extra=extra is not None,
            ties=len(ties),
        ),
        out_shape=shapes,
        in_specs=specs,
        out_specs=[vmem, hbm],
        scratch_shapes=[
            pltpu.VMEM((COLS, 2, 128, 256), BF16),
            pltpu.VMEM((2048, 256), BF16),
            pltpu.VMEM((height, 128), BF16),
            pltpu.VMEM((16, 128), F32),
            pltpu.SemaphoreType.DMA((4,)),
            pltpu.SemaphoreType.DMA((ROWS,)),
        ],
        compiler_params=PARAMS,
        cost_estimate=cost,
        name=name,
    )(
        *factors,
        *operands,
        *ties,
    )


def panel_loads(side, ids, weights, first, tile, chunk):
    total = jnp.zeros((tile, 256), F32)
    for start in range(0, 2048, chunk):
        panels = slice(start, start + chunk)
        onehot = weighted_onehot(ids[:, panels], weights[:, panels].astype(BF16), first, tile)
        total += jnp.dot(onehot, side[panels], preferred_element_type=F32)
    return total


def read_panels(gathered_ref, side):
    for source in range(ROWS):
        rows = slice(source * 128, (source + 1) * 128)
        side[rows, :128] = gathered_ref[source, :128]
        side[rows, 128:] = gathered_ref[source, 128:256]


def first_loads_kernel(gathered_ref, *rest):
    old_refs = rest[:4]
    out_ref, ids_ref, weights_ref, side, ids, weights, old, total, old_sems, sems = rest[4:]
    old_copies = [
        pltpu.make_async_copy(old_refs[j], old.at[j], old_sems.at[j]) for j in range(4)
    ]
    for copy in old_copies:
        copy.start()
    read_panels(gathered_ref, side)
    for source in range(ROWS):
        rows = slice(source * 128, (source + 1) * 128)
        notes = gathered_ref[source, 256:].astype(F32)
        for block, (to_ids, to_weights) in enumerate(((ids, weights), (ids_ref, weights_ref))):
            high, low, weight = (notes[block + k : block + k + 1] for k in (0, 2, 4))
            to_ids[:, rows] = (high * 64.0 + low).astype(jnp.int32)
            to_weights[:, rows] = weight
    for first in range(0, PATCHES, 1024):
        total[first : first + 1024] = panel_loads(side, ids, weights, first, 1024, 512)
    copies = []
    place, swap = minor_place()
    for j in range(4):
        old_copies[j].wait()
        minor = (place + j) % 4
        for major in range(4):
            block = (major * 4 + minor) + swap * 3 * (minor - major)
            rows = pl.ds(pl.multiple_of(block * 256, 256), 256)
            total[rows, :128] += old[j, major, :256].astype(F32)
            total[rows, 128:] += old[j, major, 256:].astype(F32)
            copies.append(
                pltpu.make_async_copy(total.at[rows], out_ref.at[rows], sems.at[j * 4 + major])
            )
            copies[-1].start()
    for copy in copies:
        copy.wait()


def first_loads(gathered, old):
    vmem = pl.BlockSpec(memory_space=pltpu.VMEM)
    hbm = pl.BlockSpec(memory_space=pltpu.HBM)
    return pl.pallas_call(
        first_loads_kernel,
        out_shape=(
            pltpu.HBM((PATCHES, 256), F32),
            jax.ShapeDtypeStruct((1, 2048), jnp.int32),
            jax.ShapeDtypeStruct((1, 2048), F32),
        ),
        in_specs=[vmem] + [pl.BlockSpec(memory_space=pl.ANY)] * 4,
        out_specs=(hbm, vmem, vmem),
        scratch_shapes=[
            pltpu.VMEM((2048, 256), BF16),
            pltpu.VMEM((1, 2048), jnp.int32),
            pltpu.VMEM((1, 2048), F32),
            pltpu.VMEM((4, 4, 512, 128), BF16),
            pltpu.VMEM((PATCHES, 256), F32),
            pltpu.SemaphoreType.DMA((4,)),
            pltpu.SemaphoreType.DMA((ROWS,)),
        ],
        compiler_params=PARAMS,
        cost_estimate=COST,
        name="first_loads",
    )(gathered, *old)


def all_loads_kernel(
    ids, weights, gathered_ref, first_ref, maps_ref, out_ref, held_ref, side, first, total, sem, sems
):
    first_copy = pltpu.make_async_copy(first_ref, first, sem)
    first_copy.start()
    copies = [
        pltpu.make_async_copy(maps_ref.at[k], held_ref.at[k], sems.at[k]) for k in range(COLS)
    ]
    for copy in copies:
        copy.start()
    read_panels(gathered_ref, side)
    for start in range(0, PATCHES, 1024):
        total[start : start + 1024] = panel_loads(side, ids, weights, start, 1024, 512)
    first_copy.wait()
    for start in range(0, PATCHES, 256):
        rows = slice(start, start + 256)
        out_ref[rows] = (first[rows] + total[rows]).astype(BF16)
    for copy in copies:
        copy.wait()


def all_loads(ids, weights, gathered, first, maps):
    vmem = pl.BlockSpec(memory_space=pltpu.VMEM)
    hbm = pl.BlockSpec(memory_space=pltpu.HBM)
    return pl.pallas_call(
        all_loads_kernel,
        out_shape=(pltpu.VMEM((PATCHES, 256), BF16), pltpu.VMEM(maps.shape, BF16)),
        in_specs=[vmem] * 3 + [hbm] * 2,
        out_specs=(vmem, vmem),
        scratch_shapes=[
            pltpu.VMEM((2048, 256), BF16),
            pltpu.VMEM((PATCHES, 256), F32),
            pltpu.VMEM((PATCHES, 256), F32),
            pltpu.SemaphoreType.DMA,
            pltpu.SemaphoreType.DMA((COLS,)),
        ],
        compiler_params=PARAMS,
        name="all_loads",
    )(
        ids,
        weights,
        gathered,
        pltpu.with_memory_space_constraint(first, pltpu.HBM),
        pltpu.with_memory_space_constraint(maps, pltpu.HBM),
    )


def stress_kernel(loads_ref, maps_ref, out_ref):
    for first in range(0, 1024, 512):
        rows = slice(first, first + 512)
        real = jnp.zeros((512, 256), F32)
        imag = jnp.zeros((512, 256), F32)
        for block in range(COLS):
            part = loads_ref[block * 512 : (block + 1) * 512]
            real += jnp.dot(maps_ref[block, 0, rows], part, preferred_element_type=F32)
            imag += jnp.dot(maps_ref[block, 1, rows], part, preferred_element_type=F32)
        out_ref[0, rows] = (real[:, :128] - imag[:, 128:]).astype(BF16)
        out_ref[1, rows] = (real[:, 128:] + imag[:, :128]).astype(BF16)


def stress(loads, maps):
    vmem = pl.BlockSpec(memory_space=pltpu.VMEM)
    return pl.pallas_call(
        stress_kernel,
        out_shape=jax.ShapeDtypeStruct((2, 1024, 128), BF16),
        in_specs=[vmem] * 2,
        out_specs=vmem,
        compiler_params=PARAMS,
        name="stress",
    )(
        pltpu.with_memory_space_constraint(loads, pltpu.VMEM),
        pltpu.with_memory_space_constraint(maps, pltpu.VMEM),
    )


def along_y(value, hop):
    pairs = [(i, (i // 2 + hop) % 4 * 2 + i % 2) for i in range(COLS)]
    return lax.ppermute(value, "col", pairs)


def other_core(value):
    return lax.ppermute(value, "col", [(i, i ^ 1) for i in range(COLS)])


def along_axis(value, hop, major):
    pairs = []
    for index in range(ROWS * COLS):
        x, z, rest = index // 32, index // 8 % 4, index % 8
        if major == (rest % 2 == 1):
            x = (x + hop) % 4
        else:
            z = (z + hop) % 4
        pairs.append((index, (x * 4 + z) * 8 + rest))
    return lax.ppermute(value, ("row", "col"), pairs)


def to_rows(copies):
    return lax.all_to_all(copies, "row", 0, 0, tiled=True)


def on_device(
    rhs_first,
    rhs_last,
    inv_first,
    coupling,
    inv_last,
    earlier,
    patch_old,
    weight_old,
    patch_new,
    weight_new,
    stress_map,
):
    rhs_all = to_rows(jnp.broadcast_to(rhs_first.reshape(1, 256, 128), (ROWS, 256, 128)))
    maps = lax.all_gather(stress_map, "col")
    factors = jnp.stack([inv_first, coupling, inv_last])
    factors = [factors] + [along_y(factors, hop) for hop in (1, 2, 3)]
    old = old_loads(patch_old[None], weight_old[None], earlier)
    own = list(pack_factors(factors, old[0]))
    other = [other_core(value) for value in own]
    factors = [own[:2] + other[:2], [own[2], other[2]], [own[3], other[3]]]
    x_first, copies = rows_product(
        "first_rows", factors[0], rhs_all, extra=[patch_new, weight_new], cost=BRIEF
    )
    x_first_all = to_rows(copies)
    old = [old[0]] + [along_axis(old[hop], hop, False) for hop in (1, 2, 3)]
    old = sum_loads("sum_minor", old, x_first)
    reduced, copies = rows_product(
        "reduced_rows", factors[1], x_first_all, base=rhs_last, ties=(old,)
    )
    reduced_all = to_rows(copies)
    old = [old] + [along_axis(old, hop, True) for hop in (3, 2, 1)]
    old = sum_loads("sum_major", old, reduced)
    x_last, copies = rows_product("last_rows", factors[2], reduced_all, ties=(old,))
    x_last_all = to_rows(copies)
    old = [old] + [along_axis(old, hop, False) for hop in (3, 2, 1)]
    loads, ids, weights = first_loads(x_first_all, old)
    stress_rao = stress(*all_loads(ids, weights, x_last_all, loads, maps))
    return (jnp.stack([x_first, x_last]), stress_rao)


def solution(mesh):
    in_specs = (
        P(None, "row", "col"),
        P(None, "row", "col"),
        P(None, "row", "col"),
        P(None, "row", "col"),
        P(None, "row", "col"),
        P(None, "row", "col"),
        P("row"),
        P("row"),
        P(None, "row"),
        P(None, "row"),
        P(None, "row", "col"),
    )
    out_specs = (P(None, None, "row", "col"), P(None, "row", "col"))
    return jax.shard_map(
        on_device, mesh=mesh, in_specs=in_specs, out_specs=out_specs, check_vma=False
    )
```

```python
import functools

import jax
import jax.numpy as jnp
from jax import lax
from jax.experimental import pallas as pl
from jax.experimental.pallas import tpu as pltpu
from jax.sharding import PartitionSpec as P

PATCHES = 4096
ROWS = 16
COLS = 8
BF16 = jnp.bfloat16
F32 = jnp.float32
COST = pl.CostEstimate(flops=30_000_000_000, bytes_accessed=1000, transcendentals=0)
SHORT = pl.CostEstimate(flops=6_000_000_000, bytes_accessed=1000, transcendentals=0)
BRIEF = pl.CostEstimate(flops=1_000_000_000, bytes_accessed=1000, transcendentals=0)
PARAMS = pltpu.CompilerParams(vmem_limit_bytes=20 * 2**20)


def weighted_onehot(ids, weights, first, count):
    patch = lax.broadcasted_iota(jnp.int32, (count, ids.shape[1]), 0)
    return jnp.where(patch == ids - first, weights, jnp.zeros((), BF16))


def minor_place():
    row = lax.axis_index("row")
    x, z = row // 4, row % 4
    swap = 1 - lax.axis_index("col") % 2
    return z + swap * (x - z), swap


def old_loads_kernel(ids_ref, weights_ref, earlier_ref, *rest, chunk):
    outs, side = rest[:4], rest[4]
    side[:, :128] = earlier_ref[0]
    side[:, 128:] = earlier_ref[1]
    ids = ids_ref[...]
    x, z = ids >> 10, (ids >> 8) & 3
    place, swap = minor_place()
    major = x + swap * (z - x)
    minor = z + swap * (x - z)
    labels = ((minor - place) & 3) * 1024 + major * 256 + (ids & 255)
    for k in range(4):
        total = jnp.zeros((1024, 256), F32)
        for start in range(0, side.shape[0], chunk):
            panels = slice(start, start + chunk)
            onehot = weighted_onehot(labels[:, panels], weights_ref[:, panels], k * 1024, 1024)
            total += jnp.dot(onehot, side[panels], preferred_element_type=F32)
        for block in range(4):
            rows = slice(block * 256, (block + 1) * 256)
            outs[k][block, :256] = total[rows, :128].astype(BF16)
            outs[k][block, 256:] = total[rows, 128:].astype(BF16)


def old_loads(ids, weights, earlier):
    panels = earlier.shape[1]
    vmem = pl.BlockSpec(memory_space=pltpu.VMEM)
    return pl.pallas_call(
        functools.partial(old_loads_kernel, chunk=512),
        out_shape=[jax.ShapeDtypeStruct((4, 512, 128), BF16)] * 4,
        in_specs=[vmem] * 3,
        out_specs=[vmem] * 4,
        scratch_shapes=[pltpu.VMEM((panels, 256), BF16)],
        compiler_params=PARAMS,
        name="old_loads",
    )(ids, weights, earlier)


def sum_loads_kernel(*refs):
    parts, (out_ref, held, sems) = refs[:4], refs[5:]
    copies = [
        [
            pltpu.make_async_copy(parts[k].at[block], held.at[k, block], sems.at[k, block])
            for k in range(4)
        ]
        for block in range(4)
    ]
    for block in range(4):
        for copy in copies[block]:
            copy.start()
    for block in range(4):
        for copy in copies[block]:
            copy.wait()
        total = held[0, block].astype(F32) + held[1, block].astype(F32)
        total += held[2, block].astype(F32) + held[3, block].astype(F32)
        out_ref[block] = total.astype(BF16)


def sum_loads(name, parts, tie):
    return pl.pallas_call(
        sum_loads_kernel,
        out_shape=jax.ShapeDtypeStruct(parts[0].shape, BF16),
        in_specs=[pl.BlockSpec(memory_space=pl.ANY)] * 5,
        out_specs=pl.BlockSpec(memory_space=pltpu.VMEM),
        scratch_shapes=[
            pltpu.VMEM((4, *parts[0].shape), BF16),
            pltpu.SemaphoreType.DMA((4, 4)),
        ],
        compiler_params=PARAMS,
        cost_estimate=COST,
        name=name,
    )(
        parts[0],
        *[pltpu.with_memory_space_constraint(part, pltpu.HBM) for part in parts[1:]],
        tie,
    )


def pack_factors_kernel(*refs):
    values, outs, sems = refs[:4], refs[5:9], refs[9]
    copies = []
    for k in range(4):
        targets = (outs[k // 2].at[k % 2], outs[2].at[k], outs[3].at[k])
        for m in range(3):
            copies.append(pltpu.make_async_copy(values[k].at[m], targets[m], sems.at[k, m]))
            copies[-1].start()
    for copy in copies:
        copy.wait()


def pack_factors(values, tie):
    vmem = pl.BlockSpec(memory_space=pltpu.VMEM)
    return pl.pallas_call(
        pack_factors_kernel,
        out_shape=[
            jax.ShapeDtypeStruct((count, *values[0].shape[1:]), BF16) for count in (2, 2, 4, 4)
        ],
        in_specs=[pl.BlockSpec(memory_space=pl.ANY)] * 5,
        out_specs=[vmem] * 4,
        scratch_shapes=[pltpu.SemaphoreType.DMA((4, 3))],
        compiler_params=PARAMS,
        cost_estimate=SHORT,
        name="pack_factors",
    )(
        values[0],
        *[pltpu.with_memory_space_constraint(value, pltpu.HBM) for value in values[1:]],
        tie,
    )


def send_copies(source, copies_ref, sems):
    copies = [
        pltpu.make_async_copy(source, copies_ref.at[k], sems.at[k]) for k in range(ROWS)
    ]
    for copy in copies:
        copy.start()
    for copy in copies:
        copy.wait()


def rows_kernel(*rest, parts, base, extra, ties):
    factor_refs, gathered_ref, rest = rest[:parts], rest[parts], list(rest[parts + 1 :])
    base_ref = rest.pop(0) if base else None
    ids_ref, weights_ref = (rest.pop(0), rest.pop(0)) if extra else (None, None)
    out_ref, copies_ref, factor, side, send, notes, factor_sems, sems = rest[ties:]
    size = COLS // parts
    factor_copies = [
        pltpu.make_async_copy(part_ref, factor.at[pl.ds(k * size, size)], factor_sems.at[k])
        for k, part_ref in enumerate(factor_refs)
    ]
    for copy in factor_copies:
        copy.start()
    col = lax.axis_index("col")
    core = col % 2
    for block in range(COLS):
        chip = (col // 2 + 4 - block % 4) % 4
        column = chip * 2 + (core if block < 4 else 1 - core)
        for half in range(2):
            source = column * 2 + half
            rows = slice(block * 256 + half * 128, block * 256 + (half + 1) * 128)
            side[rows, :128] = gathered_ref[source, :128]
            side[rows, 128:] = gathered_ref[source, 128:256]
    total = jnp.zeros((256, 256), F32)
    for copy in factor_copies:
        copy.wait()
    for block in range(COLS):
        part = side[block * 256 : (block + 1) * 256]
        left = factor[block].reshape(256, 256)
        total += jnp.dot(left, part, preferred_element_type=F32)
    out_real = total[:128, :128] - total[128:, 128:]
    out_imag = total[:128, 128:] + total[128:, :128]
    if base:
        out_real = base_ref[0].astype(F32) - out_real
        out_imag = base_ref[1].astype(F32) - out_imag
    out_real = out_real.astype(BF16)
    out_imag = out_imag.astype(BF16)
    out_ref[0] = out_real
    out_ref[1] = out_imag
    send[:128] = out_real
    send[128:256] = out_imag
    if extra:
        notes[...] = jnp.zeros_like(notes)
        ids = ids_ref[...]
        notes[0:2] = (ids >> 6).astype(F32)
        notes[2:4] = (ids & 63).astype(F32)
        notes[4:6] = weights_ref[...].astype(F32)
        send[256:] = notes[...].astype(BF16)
    send_copies(send, copies_ref, sems)


def rows_product(name, factors, gathered, base=None, extra=None, ties=(), cost=COST):
    vmem = pl.BlockSpec(memory_space=pltpu.VMEM)
    hbm = pl.BlockSpec(memory_space=pltpu.HBM)
    operands = [gathered]
    operands += [] if base is None else [base]
    operands += [] if extra is None else extra
    specs = [pl.BlockSpec(memory_space=pl.ANY)] * len(factors) + [vmem] * len(operands)
    specs += [pl.BlockSpec(memory_space=pl.ANY)] * len(ties)
    height = 256 if extra is None else 272
    shapes = [jax.ShapeDtypeStruct((2, 128, 128), BF16), pltpu.HBM((ROWS, height, 128), BF16)]
    return pl.pallas_call(
        functools.partial(
            rows_kernel,
            parts=len(factors),
            base=base is not None,
            extra=extra is not None,
            ties=len(ties),
        ),
        out_shape=shapes,
        in_specs=specs,
        out_specs=[vmem, hbm],
        scratch_shapes=[
            pltpu.VMEM((COLS, 2, 128, 256), BF16),
            pltpu.VMEM((2048, 256), BF16),
            pltpu.VMEM((height, 128), BF16),
            pltpu.VMEM((16, 128), F32),
            pltpu.SemaphoreType.DMA((4,)),
            pltpu.SemaphoreType.DMA((ROWS,)),
        ],
        compiler_params=PARAMS,
        cost_estimate=cost,
        name=name,
    )(
        *factors,
        *operands,
        *ties,
    )


def panel_loads(side, ids, weights, first, tile, chunk):
    total = jnp.zeros((tile, 256), F32)
    for start in range(0, 2048, chunk):
        panels = slice(start, start + chunk)
        onehot = weighted_onehot(ids[:, panels], weights[:, panels].astype(BF16), first, tile)
        total += jnp.dot(onehot, side[panels], preferred_element_type=F32)
    return total


def read_panels(gathered_ref, side):
    for source in range(ROWS):
        rows = slice(source * 128, (source + 1) * 128)
        side[rows, :128] = gathered_ref[source, :128]
        side[rows, 128:] = gathered_ref[source, 128:256]


def first_loads_kernel(gathered_ref, *rest):
    old_refs = rest[:4]
    out_ref, ids_ref, weights_ref, side, ids, weights, old, total, old_sems, sems = rest[4:]
    old_copies = [
        pltpu.make_async_copy(old_refs[j], old.at[j], old_sems.at[j]) for j in range(4)
    ]
    for copy in old_copies:
        copy.start()
    read_panels(gathered_ref, side)
    for source in range(ROWS):
        rows = slice(source * 128, (source + 1) * 128)
        notes = gathered_ref[source, 256:].astype(F32)
        for block, (to_ids, to_weights) in enumerate(((ids, weights), (ids_ref, weights_ref))):
            high, low, weight = (notes[block + k : block + k + 1] for k in (0, 2, 4))
            to_ids[:, rows] = (high * 64.0 + low).astype(jnp.int32)
            to_weights[:, rows] = weight
    for first in range(0, PATCHES, 1024):
        total[first : first + 1024] = panel_loads(side, ids, weights, first, 1024, 512)
    copies = []
    place, swap = minor_place()
    for j in range(4):
        old_copies[j].wait()
        minor = (place + j) % 4
        for major in range(4):
            block = (major * 4 + minor) + swap * 3 * (minor - major)
            rows = pl.ds(pl.multiple_of(block * 256, 256), 256)
            total[rows, :128] += old[j, major, :256].astype(F32)
            total[rows, 128:] += old[j, major, 256:].astype(F32)
            copies.append(
                pltpu.make_async_copy(total.at[rows], out_ref.at[rows], sems.at[j * 4 + major])
            )
            copies[-1].start()
    for copy in copies:
        copy.wait()


def first_loads(gathered, old):
    vmem = pl.BlockSpec(memory_space=pltpu.VMEM)
    hbm = pl.BlockSpec(memory_space=pltpu.HBM)
    return pl.pallas_call(
        first_loads_kernel,
        out_shape=(
            pltpu.HBM((PATCHES, 256), F32),
            jax.ShapeDtypeStruct((1, 2048), jnp.int32),
            jax.ShapeDtypeStruct((1, 2048), F32),
        ),
        in_specs=[vmem] + [pl.BlockSpec(memory_space=pl.ANY)] * 4,
        out_specs=(hbm, vmem, vmem),
        scratch_shapes=[
            pltpu.VMEM((2048, 256), BF16),
            pltpu.VMEM((1, 2048), jnp.int32),
            pltpu.VMEM((1, 2048), F32),
            pltpu.VMEM((4, 4, 512, 128), BF16),
            pltpu.VMEM((PATCHES, 256), F32),
            pltpu.SemaphoreType.DMA((4,)),
            pltpu.SemaphoreType.DMA((ROWS,)),
        ],
        compiler_params=PARAMS,
        cost_estimate=COST,
        name="first_loads",
    )(gathered, *old)


def all_loads_kernel(
    ids, weights, gathered_ref, first_ref, maps_ref, out_ref, held_ref, side, first, total, sem, sems
):
    first_copy = pltpu.make_async_copy(first_ref, first, sem)
    first_copy.start()
    copies = [
        pltpu.make_async_copy(maps_ref.at[k], held_ref.at[k], sems.at[k]) for k in range(COLS)
    ]
    for copy in copies:
        copy.start()
    read_panels(gathered_ref, side)
    for start in range(0, PATCHES, 1024):
        total[start : start + 1024] = panel_loads(side, ids, weights, start, 1024, 512)
    first_copy.wait()
    for start in range(0, PATCHES, 256):
        rows = slice(start, start + 256)
        out_ref[rows] = (first[rows] + total[rows]).astype(BF16)
    for copy in copies:
        copy.wait()


def all_loads(ids, weights, gathered, first, maps):
    vmem = pl.BlockSpec(memory_space=pltpu.VMEM)
    hbm = pl.BlockSpec(memory_space=pltpu.HBM)
    return pl.pallas_call(
        all_loads_kernel,
        out_shape=(pltpu.VMEM((PATCHES, 256), BF16), pltpu.VMEM(maps.shape, BF16)),
        in_specs=[vmem] * 3 + [hbm] * 2,
        out_specs=(vmem, vmem),
        scratch_shapes=[
            pltpu.VMEM((2048, 256), BF16),
            pltpu.VMEM((PATCHES, 256), F32),
            pltpu.VMEM((PATCHES, 256), F32),
            pltpu.SemaphoreType.DMA,
            pltpu.SemaphoreType.DMA((COLS,)),
        ],
        compiler_params=PARAMS,
        name="all_loads",
    )(
        ids,
        weights,
        gathered,
        pltpu.with_memory_space_constraint(first, pltpu.HBM),
        pltpu.with_memory_space_constraint(maps, pltpu.HBM),
    )


def stress_kernel(loads_ref, maps_ref, out_ref):
    for first in range(0, 1024, 512):
        rows = slice(first, first + 512)
        real = jnp.zeros((512, 256), F32)
        imag = jnp.zeros((512, 256), F32)
        for block in range(COLS):
            part = loads_ref[block * 512 : (block + 1) * 512]
            real += jnp.dot(maps_ref[block, 0, rows], part, preferred_element_type=F32)
            imag += jnp.dot(maps_ref[block, 1, rows], part, preferred_element_type=F32)
        out_ref[0, rows] = (real[:, :128] - imag[:, 128:]).astype(BF16)
        out_ref[1, rows] = (real[:, 128:] + imag[:, :128]).astype(BF16)


def stress(loads, maps):
    vmem = pl.BlockSpec(memory_space=pltpu.VMEM)
    return pl.pallas_call(
        stress_kernel,
        out_shape=jax.ShapeDtypeStruct((2, 1024, 128), BF16),
        in_specs=[vmem] * 2,
        out_specs=vmem,
        compiler_params=PARAMS,
        name="stress",
    )(
        pltpu.with_memory_space_constraint(loads, pltpu.VMEM),
        pltpu.with_memory_space_constraint(maps, pltpu.VMEM),
    )


def along_y(value, hop):
    pairs = [(i, (i // 2 + hop) % 4 * 2 + i % 2) for i in range(COLS)]
    return lax.ppermute(value, "col", pairs)


def other_core(value):
    return lax.ppermute(value, "col", [(i, i ^ 1) for i in range(COLS)])


def along_axis(value, hop, major):
    pairs = []
    for index in range(ROWS * COLS):
        x, z, rest = index // 32, index // 8 % 4, index % 8
        if major == (rest % 2 == 1):
            x = (x + hop) % 4
        else:
            z = (z + hop) % 4
        pairs.append((index, (x * 4 + z) * 8 + rest))
    return lax.ppermute(value, ("row", "col"), pairs)


def to_rows(copies):
    return lax.all_to_all(copies, "row", 0, 0, tiled=True)


def on_device(
    rhs_first,
    rhs_last,
    inv_first,
    coupling,
    inv_last,
    earlier,
    patch_old,
    weight_old,
    patch_new,
    weight_new,
    stress_map,
):
    rhs_all = to_rows(jnp.broadcast_to(rhs_first.reshape(1, 256, 128), (ROWS, 256, 128)))
    maps = lax.all_gather(stress_map, "col")
    factors = jnp.stack([inv_first, coupling, inv_last])
    factors = [factors] + [along_y(factors, hop) for hop in (1, 2, 3)]
    old = old_loads(patch_old[None], weight_old[None], earlier)
    own = list(pack_factors(factors, old[0]))
    other = [other_core(value) for value in own]
    factors = [own[:2] + other[:2], [own[2], other[2]], [own[3], other[3]]]
    x_first, copies = rows_product(
        "first_rows", factors[0], rhs_all, extra=[patch_new, weight_new], cost=BRIEF
    )
    x_first_all = to_rows(copies)
    old = [old[0]] + [along_axis(old[hop], hop, False) for hop in (1, 2, 3)]
    old = sum_loads("sum_minor", old, x_first)
    reduced, copies = rows_product(
        "reduced_rows", factors[1], x_first_all, base=rhs_last, ties=(old,)
    )
    reduced_all = to_rows(copies)
    old = [old] + [along_axis(old, hop, True) for hop in (3, 2, 1)]
    old = sum_loads("sum_major", old, reduced)
    x_last, copies = rows_product("last_rows", factors[2], reduced_all, ties=(old,))
    x_last_all = to_rows(copies)
    old = [old] + [along_axis(old, hop, False) for hop in (3, 2, 1)]
    loads, ids, weights = first_loads(x_first_all, old)
    stress_rao = stress(*all_loads(ids, weights, x_last_all, loads, maps))
    return (jnp.stack([x_first, x_last]), stress_rao)


def solution(mesh):
    in_specs = (
        P(None, "row", "col"),
        P(None, "row", "col"),
        P(None, "row", "col"),
        P(None, "row", "col"),
        P(None, "row", "col"),
        P(None, "row", "col"),
        P("row"),
        P("row"),
        P(None, "row"),
        P(None, "row"),
        P(None, "row", "col"),
    )
    out_specs = (P(None, None, "row", "col"), P(None, "row", "col"))
    return jax.shard_map(
        on_device, mesh=mesh, in_specs=in_specs, out_specs=out_specs, check_vma=False
    )
```
